32 devices in a mesh: group: 16 (over z, y, core), tensor: 2 (over x).
Axes of the slice: x: 2, y: 2, z: 4, core: 2. Of those that a mesh axis runs over, the one named last changes fastest.
Arguments:
- new_q: bfloat16 [8192, 5120], P('group', 'tensor'), may hold values from -420 to 420
- new_k: bfloat16 [8192, 5120], P('group', 'tensor'), may hold values from -420 to 420
- new_v: bfloat16 [8192, 5120], P('group', 'tensor'), may hold values from -6 to 6
- cache_k: bfloat16 [14336, 5120], P('group', 'tensor'), may hold values from -30 to 30
- cache_v: bfloat16 [14336, 5120], P('group', 'tensor'), may hold values from -6 to 6
- q_gain: float32 [5120], P('tensor'), may hold values from 1 to 3
- k_gain: float32 [5120], P('tensor'), may hold values from 1 to 3
- cache_len: int32 [16], replicated, may hold values from 2 to 1664, as said below
- home_blocks: int32 [16], replicated, may hold values from 1 to 7, as said below
Outputs:
- attended: bfloat16 [8192, 5120], P('group', 'tensor')
The draws below stay inside these ranges and needn't reach their ends.
Inputs may be any that keep to these rules, and one draw needn't show every extreme that they name: ceil(cache_len / 128) of a request and of its partner (index XOR 1) sum to at most 14. home_blocks[r] = min(ceil(cache_len[r] / 128), 7).
All inputs are finite; a program needn't handle non-finite values.
Results may differ from the reference program's by a relative error of at most 0.03.
Values may be sent and summed in bfloat16 or wider, within the bound.
No kernel may reach another device: no remote copies, remote signals or barrier semaphores. Data moves between devices by JAX's collectives and lax.ppermute only.
A program may use at most 192 MiB of HBM per device.

```python
import math
import jax
import jax.numpy as jnp
from jax import lax

HEADS = 40
HD = 128
NEW = 512
SLOTS = 7
CB = 128
REQUESTS = 16
D = 5120
TOKENS = 8192
CACHED = 14336


def head_of_column():
    return jnp.arange(HEADS * HD, dtype=jnp.int32) // HD


def column_scale(sub_key, low_end, high_end):
    rising = 3.0 ** (head_of_column().astype(jnp.float32) / max(HEADS - 1, 1))
    return rising * jax.random.uniform(sub_key, (HEADS * HD,), jnp.float32, low_end, high_end)


def raw_field(sub_key, row_count):
    return jnp.clip(jax.random.normal(jax.random.fold_in(sub_key, 1), (row_count, HEADS * HD), jnp.float32), -4.0, 4.0)


def projected(key, salt):
    row_count = REQUESTS * NEW
    sub_key = jax.random.fold_in(key, salt)
    baseline = raw_field(jax.random.fold_in(sub_key, 3), row_count)
    row_scale = jnp.exp(jax.random.uniform(jax.random.fold_in(sub_key, 4), (row_count, 1), jnp.float32, 0.0, math.log(10.0)))
    return baseline * row_scale * column_scale(jax.random.fold_in(sub_key, 5), 1.0, 3.4)[None, :]


def draw_new_q(key, part):
    values = projected(key, 10)
    return values.astype(jnp.bfloat16)


def draw_new_k(key, part):
    return projected(key, 20).astype(jnp.bfloat16)


def draw_cache_k(key, part):
    row_count = REQUESTS * SLOTS * CB
    sub_key = jax.random.fold_in(key, 30)
    values = raw_field(jax.random.fold_in(sub_key, 1), row_count) * column_scale(jax.random.fold_in(sub_key, 2), 0.6, 1.8)[None, :]
    return values.astype(jnp.bfloat16)


def request_blocks(key):
    pair_count = REQUESTS // 2
    block_span = 2 * SLOTS
    first_blocks = jax.random.randint(jax.random.fold_in(key, 40), (pair_count,), 1, block_span)
    second_blocks = 1 + jax.random.randint(jax.random.fold_in(key, 41), (pair_count,), 0, 1 << 20) % (block_span - first_blocks)
    chosen_pair = jnp.arange(pair_count, dtype=jnp.int32) == jax.random.randint(jax.random.fold_in(key, 42), (), 0, pair_count)
    first_blocks = jnp.where(chosen_pair, block_span - 1, first_blocks)
    second_blocks = jnp.where(chosen_pair, 1, second_blocks)
    flipped = jax.random.randint(jax.random.fold_in(key, 43), (pair_count,), 0, 2) == 1
    left_blocks = jnp.where(flipped, second_blocks, first_blocks)
    right_blocks = jnp.where(flipped, first_blocks, second_blocks)
    blocks = jnp.stack([left_blocks, right_blocks], axis=1).reshape(REQUESTS)
    tail_tokens = jax.random.randint(jax.random.fold_in(key, 44), (REQUESTS,), 2, CB + 1)
    longest = jnp.repeat(chosen_pair, 2) & (blocks == block_span - 1)
    tail_tokens = jnp.where(longest, CB, tail_tokens)
    return (blocks, (blocks - 1) * CB + tail_tokens)


def draw_cache_len(key, part):
    return request_blocks(key)[1].astype(jnp.int32)


def draw_home_blocks(key, part):
    return jnp.minimum(request_blocks(key)[0], SLOTS).astype(jnp.int32)


def level_of(rng, shape, cuts, low, high):
    factor_of, own = 1.0, jax.random.fold_in(rng, 6)
    for axis_at, blocks in cuts:
        draws = jnp.exp(jax.random.uniform(jax.random.fold_in(own, axis_at), (blocks,), jnp.float32, low / len(cuts), high / len(cuts)))
        factor_of = factor_of * jnp.repeat(draws, shape[axis_at] // blocks).reshape([-1 if axis == axis_at else 1 for axis in range(len(shape))])
    return factor_of


def normal_values(key, shape, deviation, reach, split=(), kind=jnp.bfloat16):
    factor_of = level_of(key, shape, split, -0.22, 0.18) if split else 1.0
    values = jax.random.normal(key, shape, jnp.float32) * deviation * factor_of
    return jnp.minimum(jnp.maximum(values, -reach), reach).astype(kind)


def setup_inputs(seed: int = 0) -> dict:
    arg_keys = jax.random.split(jax.random.key(seed), 10)
    return {
        "new_q": draw_new_q(jax.random.fold_in(arg_keys[9], 71), 0),
        "new_k": draw_new_k(jax.random.fold_in(arg_keys[9], 71), 0),
        "new_v": normal_values(arg_keys[2], (TOKENS, D), 1.0, 6.0, ((0, 16), (1, 2))),
        "cache_k": draw_cache_k(jax.random.fold_in(arg_keys[9], 71), 0),
        "cache_v": normal_values(arg_keys[4], (CACHED, D), 1.0, 6.0, ((0, 16), (1, 2))),
        "q_gain": jnp.clip(jnp.exp(math.log(3.0) - 1.0986123 * jax.random.uniform(arg_keys[5], (D,), jnp.float32) ** level_of(arg_keys[5], (D,), ((0, 2),), -0.2, 0.2)), 1.0, 3.0),
        "k_gain": jnp.clip(jnp.exp(math.log(3.0) - 1.0986123 * jax.random.uniform(arg_keys[6], (D,), jnp.float32) ** level_of(arg_keys[6], (D,), ((0, 2),), -0.2, 0.2)), 1.0, 3.0),
        "cache_len": draw_cache_len(jax.random.fold_in(arg_keys[9], 71), 0),
        "home_blocks": draw_home_blocks(jax.random.fold_in(arg_keys[9], 71), 0),
    }


def rms_normed(source, scaling):
    widened = source.astype(jnp.float32)
    mean_square = lax.optimization_barrier(jnp.mean(widened * widened, axis=1, keepdims=True))
    return (widened * lax.rsqrt(mean_square + 1e-06) * scaling).astype(jnp.bfloat16)

def reference(new_q, new_k, new_v, cache_k, cache_v, q_gain, k_gain, cache_len, home_blocks):
    feature_count = HEADS * HD
    q_normed = rms_normed(new_q, q_gain).reshape(REQUESTS, NEW, HEADS, HD)
    k_normed = rms_normed(new_k, k_gain).reshape(REQUESTS, NEW, HEADS, HD)
    fresh_values = new_v.reshape(REQUESTS, NEW, HEADS, HD)
    stored_keys = cache_k.reshape(REQUESTS, SLOTS * CB, HEADS, HD)
    stored_values = cache_v.reshape(REQUESTS, SLOTS * CB, HEADS, HD)
    blocks = (cache_len + CB - 1) // CB
    tokens = jnp.arange(SLOTS * CB, dtype=jnp.int32)
    slot_index = tokens // CB
    within = tokens % CB

    def attend_request(request):
        partner = jnp.bitwise_xor(request, 1)
        length = cache_len[request]
        home_count = home_blocks[request]
        partner_home = home_blocks[partner]
        own_ok = (slot_index < home_count) & (tokens < length)
        block_index = slot_index - partner_home + home_count
        far_ok = (slot_index >= partner_home) & (block_index < blocks[request]) & (block_index * CB + within < length)
        key_rows = jnp.concatenate([stored_keys[request], stored_keys[partner], k_normed[request]], axis=0).astype(jnp.float32)
        value_rows = jnp.concatenate([stored_values[request], stored_values[partner], fresh_values[request]], axis=0).astype(jnp.float32)
        usable = jnp.concatenate([own_ok, far_ok, jnp.ones((NEW,), jnp.bool_)])
        queries = q_normed[request].astype(jnp.float32)
        scores = jnp.einsum('qhd,khd->hqk', queries, key_rows) * HD ** (-0.5)
        scores = jnp.where(usable[None, None, :], scores, -1e+30)
        row_top = lax.optimization_barrier(jnp.max(scores, axis=2, keepdims=True))
        weights = jnp.where(usable[None, None, :], jnp.exp(scores - row_top), 0.0)
        totals = lax.optimization_barrier(jnp.sum(weights, axis=2))
        rounded = lax.optimization_barrier(weights.astype(jnp.bfloat16)).astype(jnp.float32)
        mixture = jnp.einsum('hqk,khd->qhd', rounded, value_rows) / jnp.transpose(totals)[:, :, None]
        return mixture.astype(jnp.bfloat16).reshape(NEW, feature_count)
    result = lax.map(attend_request, jnp.arange(REQUESTS, dtype=jnp.int32))
    return result.reshape(REQUESTS * NEW, feature_count)
```

```python
import functools
import math

import jax
import jax.numpy as jnp
from jax import lax
from jax.experimental import pallas as pl
from jax.experimental.pallas import tpu as pltpu
from jax.sharding import PartitionSpec as P

HEADS = 40
HD = 128
CB = 128
EPS = 1e-06
NEGATIVE = -1e30
SCALE = math.log2(math.e) / math.sqrt(HD)
ROWS = 256
VMEM = 56 * 1024 * 1024


def swap_pairs(count):
    return [(source, source ^ 1) for source in range(count)]


def row_scale(square, width, factor):
    scale = lax.rsqrt(square / width + EPS) * factor
    pieces = []
    for start in range(0, square.shape[1], HD):
        piece = jnp.broadcast_to(scale[:, start : start + HD], (HD, HD))
        pieces.append(jnp.transpose(piece))
    return jnp.concatenate(pieces, axis=0)


def scores_of(queries, keys):
    return lax.dot_general(
        queries, keys, (((1,), (1,)), ((), ())), preferred_element_type=jnp.float32
    )


def columns_of(scores, tail=None):
    count = scores.shape[1] // CB
    columns = [scores[:, i * CB : (i + 1) * CB] for i in range(count)]
    if tail is not None:
        lane = lax.broadcasted_iota(jnp.int32, columns[-1].shape, 1)
        columns[-1] = jnp.where(lane < tail, columns[-1], NEGATIVE)
    return columns


def largest(columns):
    top = columns[0]
    for column in columns[1:]:
        top = jnp.maximum(top, column)
    return jnp.max(top, axis=1, keepdims=True)


def weights_of(columns, top):
    return jnp.concatenate([jnp.exp2(c - top).astype(jnp.bfloat16) for c in columns], axis=1)


def mixed(weights, values):
    wide = jnp.concatenate([values, jnp.ones_like(values)], axis=1)
    return jnp.dot(weights, wide, preferred_element_type=jnp.float32)


def attend(head_count, row_count, queries_of, parts_of, finish):
    units = [(head, start) for head in range(head_count) for start in range(0, row_count, ROWS)]
    parts = {}

    def score(unit):
        head, start = unit
        if head not in parts:
            parts[head] = parts_of(head)
        queries = queries_of(head, start)
        return [scores_of(queries, keys) for keys, _, _ in parts[head]]

    ahead = score(units[0])
    for index, unit in enumerate(units):
        now = ahead
        if index + 1 < len(units):
            ahead = score(units[index + 1])
        head, start = unit
        split = [columns_of(s, tail) for s, (_, _, tail) in zip(now, parts[head])]
        top = largest([c for columns in split for c in columns])
        total = None
        for columns, (_, values, _) in zip(split, parts[head]):
            piece = mixed(weights_of(columns, top), values)
            total = piece if total is None else total + piece
        finish(head, start, total[:, :HD], top, total[:, HD:])


def counts(me_ref, len_ref, home_ref, slots):
    me = me_ref[0]
    partner = jnp.bitwise_xor(me, 1)
    own_home = jnp.clip(home_ref[me], 1, slots)
    own_blocks = (len_ref[me] + CB - 1) // CB
    far_home = jnp.clip(home_ref[partner], 1, slots)
    far_blocks = (len_ref[partner] + CB - 1) // CB
    own_tail = jnp.minimum(len_ref[me] - (own_home - 1) * CB, CB)
    far_count = jnp.clip(far_blocks - far_home, 0, slots - own_home)
    far_tail = len_ref[partner] - (far_blocks - 1) * CB
    return own_home, own_tail, far_count, far_tail, own_blocks > own_home


def column_slice(head):
    return slice(head * HD, (head + 1) * HD)


def far_kernel(
    me_ref, len_ref, home_ref, q_ref, k_ref, v_ref, gain_ref, square_ref, out_ref, top_ref, sum_ref, scale_ref,
    *, slots, heads_step
):
    step = pl.program_id(0)
    own_home, _, far_count, far_tail, _ = counts(me_ref, len_ref, home_ref, slots)
    row_count = q_ref.shape[0]

    @pl.when((step == 0) & (far_count > 0))
    def _():
        scale_ref[...] = row_scale(square_ref[...], HEADS * HD, SCALE)

    for count in range(1, slots):

        @pl.when(far_count == count)
        def _():
            first = pl.multiple_of(jnp.minimum(own_home, slots - count) * CB, CB)
            rows = pl.ds(first, count * CB)
            lane = lax.broadcasted_iota(jnp.int32, (ROWS, HD), 1)

            def queries_of(head, start):
                piece = pl.ds(start, ROWS)
                raw = q_ref[piece, column_slice(head)].astype(jnp.float32)
                return (raw * scale_ref[piece, :] * gain_ref[:, column_slice(head)]).astype(jnp.bfloat16)

            def parts_of(head):
                return [(k_ref[rows, column_slice(head)], v_ref[rows, column_slice(head)], far_tail)]

            def finish(head, start, mixture, top, total):
                piece = pl.ds(start, ROWS)
                out_ref[piece, column_slice(head)] = (mixture / total).astype(jnp.bfloat16)
                here = lane == step * heads_step + head
                pltpu.store(top_ref.at[piece, :], jnp.broadcast_to(top, (ROWS, HD)), mask=here)
                pltpu.store(sum_ref.at[piece, :], total, mask=here)

            attend(heads_step, row_count, queries_of, parts_of, finish)


def own_kernel(
    me_ref, len_ref, home_ref, q_ref, k_ref, v_ref, nk_ref, nv_ref, qg_ref, kg_ref, qs_ref, ks_ref,
    out_ref, top_ref, sum_ref, q_scale_ref, k_scale_ref, *, slots, heads_step
):
    step = pl.program_id(0)
    own_home, own_tail, _, _, _ = counts(me_ref, len_ref, home_ref, slots)
    row_count = q_ref.shape[0]

    @pl.when(step == 0)
    def _():
        q_scale_ref[...] = row_scale(qs_ref[...], HEADS * HD, SCALE)
        k_scale_ref[...] = row_scale(ks_ref[...], HEADS * HD, 1.0)

    for count in range(1, slots + 1):

        @pl.when(own_home == count)
        def _():
            lane = lax.broadcasted_iota(jnp.int32, (ROWS, HD), 1)

            def queries_of(head, start):
                piece = pl.ds(start, ROWS)
                raw = q_ref[piece, column_slice(head)].astype(jnp.float32)
                return (raw * q_scale_ref[piece, :] * qg_ref[:, column_slice(head)]).astype(jnp.bfloat16)

            def parts_of(head):
                raw = nk_ref[:, column_slice(head)].astype(jnp.float32)
                fresh = (raw * k_scale_ref[...] * kg_ref[:, column_slice(head)]).astype(jnp.bfloat16)
                rows = pl.ds(0, count * CB)
                return [
                    (k_ref[rows, column_slice(head)], v_ref[rows, column_slice(head)], own_tail),
                    (fresh, nv_ref[:, column_slice(head)], None),
                ]

            def finish(head, start, mixture, top, total):
                piece = pl.ds(start, ROWS)
                out_ref[piece, column_slice(head)] = (mixture / total).astype(jnp.bfloat16)
                here = lane == step * heads_step + head
                pltpu.store(top_ref.at[piece, :], jnp.broadcast_to(top, (ROWS, HD)), mask=here)
                pltpu.store(sum_ref.at[piece, :], total, mask=here)

            attend(heads_step, row_count, queries_of, parts_of, finish)


def join_kernel(
    me_ref, len_ref, home_ref, own_ref, far_ref, top_ref, sum_ref, far_top_ref, far_sum_ref, out_ref, *, slots
):
    has_far = counts(me_ref, len_ref, home_ref, slots)[4]

    @pl.when(has_far)
    def _():
        top = jnp.maximum(top_ref[...], far_top_ref[...])
        own_part = sum_ref[...] * jnp.exp2(top_ref[...] - top)
        far_part = far_sum_ref[...] * jnp.exp2(far_top_ref[...] - top)
        share = far_part / (own_part + far_part)
        for head in range(own_ref.shape[1] // HD):
            own = own_ref[:, column_slice(head)].astype(jnp.float32)
            far = far_ref[:, column_slice(head)].astype(jnp.float32)
            out_ref[:, column_slice(head)] = (own + share[:, head : head + 1] * (far - own)).astype(jnp.bfloat16)

    @pl.when(jnp.logical_not(has_far))
    def _():
        out_ref[...] = own_ref[...]


def params():
    return pltpu.CompilerParams(vmem_limit_bytes=VMEM, dimension_semantics=("arbitrary",))


def body(groups, tensors, new_q, new_k, new_v, cache_k, cache_v, q_gain, k_gain, cache_len, home_blocks):
    row_count, feature_count = new_q.shape
    heads_here = feature_count // HD
    slot_rows = cache_k.shape[0]
    slots = slot_rows // CB
    heads_step = 2 if heads_here % 2 == 0 else 1
    steps = heads_here // heads_step
    wide = heads_step * HD

    far_q = lax.ppermute(new_q, "group", swap_pairs(groups))
    wide_q = new_q.astype(jnp.float32)
    wide_k = new_k.astype(jnp.float32)
    squares = jnp.stack([jnp.sum(wide_q * wide_q, axis=1), jnp.sum(wide_k * wide_k, axis=1)])
    if tensors == 2:
        diagonal = [(source, source ^ 3) for source in range(groups * tensors)]
        other = lax.ppermute(squares, "tensor", swap_pairs(tensors))
        far_square = lax.ppermute(squares, "group", swap_pairs(groups)) + lax.ppermute(
            squares, ("group", "tensor"), diagonal
        )
        squares = squares + other
    else:
        squares = lax.psum(squares, "tensor")
        far_square = lax.ppermute(squares, "group", swap_pairs(groups))
    q_square, k_square, far_square = squares[0:1], squares[1:2], far_square[0:1]

    me = lax.axis_index("group").astype(jnp.int32).reshape(1)
    q_gain = q_gain.reshape(1, feature_count)
    k_gain = k_gain.reshape(1, feature_count)
    scalars = (me, cache_len, home_blocks)

    def skip(me_ref, len_ref, home_ref, step):
        return jnp.where(counts(me_ref, len_ref, home_ref, slots)[2] > 0, step, 0)

    def column(rows, far=False):
        if far:
            return pl.BlockSpec((rows, wide), lambda i, *s: (0, skip(*s, i)))
        return pl.BlockSpec((rows, wide), lambda i, *s: (0, i))

    def whole(*shape):
        return pl.BlockSpec(shape, lambda i, *s: (0, 0))

    stat = jax.ShapeDtypeStruct((row_count, HD), jnp.float32)
    result = jax.ShapeDtypeStruct((row_count, feature_count), jnp.bfloat16)
    pairs = row_count * heads_here * CB
    far_out, far_top, far_sum = pl.pallas_call(
        functools.partial(far_kernel, slots=slots, heads_step=heads_step),
        out_shape=(result, stat, stat),
        grid_spec=pltpu.PrefetchScalarGridSpec(
            num_scalar_prefetch=3,
            grid=(steps,),
            in_specs=[
                column(row_count, True),
                column(slot_rows, True),
                column(slot_rows, True),
                column(1, True),
                whole(1, row_count),
            ],
            out_specs=(column(row_count, True), whole(row_count, HD), whole(row_count, HD)),
            scratch_shapes=[pltpu.VMEM((row_count, HD), jnp.float32)],
        ),
        compiler_params=params(),
        cost_estimate=pl.CostEstimate(
            flops=4 * pairs * HD * 6, bytes_accessed=2 * slot_rows * feature_count * 2, transcendentals=pairs * 6
        ),
        name="far_attention",
    )(*scalars, far_q, cache_k, cache_v, q_gain, far_square)
    back = lax.ppermute((far_out, far_top, far_sum), "group", swap_pairs(groups))

    own_out, own_top, own_sum = pl.pallas_call(
        functools.partial(own_kernel, slots=slots, heads_step=heads_step),
        out_shape=(result, stat, stat),
        grid_spec=pltpu.PrefetchScalarGridSpec(
            num_scalar_prefetch=3,
            grid=(steps,),
            in_specs=[
                column(row_count),
                column(slot_rows),
                column(slot_rows),
                column(row_count),
                column(row_count),
                column(1),
                column(1),
                whole(1, row_count),
                whole(1, row_count),
            ],
            out_specs=(column(row_count), whole(row_count, HD), whole(row_count, HD)),
            scratch_shapes=[pltpu.VMEM((row_count, HD), jnp.float32)] * 2,
        ),
        compiler_params=params(),
        cost_estimate=pl.CostEstimate(
            flops=4 * pairs * HD * 8, bytes_accessed=3 * slot_rows * feature_count * 2, transcendentals=pairs * 8
        ),
        name="own_attention",
    )(*scalars, new_q, cache_k, cache_v, new_k, new_v, q_gain, k_gain, q_square, k_square)

    join_rows = 64
    wide_rows = pl.BlockSpec((join_rows, feature_count), lambda i, *s: (i, 0))
    stat_rows = pl.BlockSpec((join_rows, HD), lambda i, *s: (i, 0))
    return pl.pallas_call(
        functools.partial(join_kernel, slots=slots),
        out_shape=result,
        grid_spec=pltpu.PrefetchScalarGridSpec(
            num_scalar_prefetch=3,
            grid=(row_count // join_rows,),
            in_specs=[wide_rows, wide_rows, stat_rows, stat_rows, stat_rows, stat_rows],
            out_specs=wide_rows,
        ),
        compiler_params=params(),
        name="join_parts",
    )(*scalars, own_out, back[0], own_top, own_sum, back[1], back[2])


def solution(mesh):
    placed = (
        P("group", "tensor"),
        P("group", "tensor"),
        P("group", "tensor"),
        P("group", "tensor"),
        P("group", "tensor"),
        P("tensor"),
        P("tensor"),
        P(),
        P(),
    )
    return jax.shard_map(
        functools.partial(body, mesh.shape["group"], mesh.shape["tensor"]),
        mesh=mesh,
        in_specs=placed,
        out_specs=P("group", "tensor"),
        check_vma=False,
    )
```

```python
import functools
import math

import jax
import jax.numpy as jnp
from jax import lax
from jax.experimental import pallas as pl
from jax.experimental.pallas import tpu as pltpu
from jax.sharding import PartitionSpec as P

HEADS = 40
HD = 128
CB = 128
EPS = 1e-06
NEGATIVE = -1e30
SCALE = math.log2(math.e) / math.sqrt(HD)
SUM_LANE = 64
VMEM = 40 * 1024 * 1024


def swap_pairs(count):
    return [(source, source ^ 1) for source in range(count)]


def row_scale(square, width, factor):
    scale = lax.rsqrt(square / width + EPS) * factor
    pieces = []
    for start in range(0, square.shape[1], HD):
        piece = jnp.broadcast_to(scale[:, start : start + HD], (HD, HD))
        pieces.append(jnp.transpose(piece))
    return jnp.concatenate(pieces, axis=0)


def counts(me_ref, len_ref, home_ref, slots):
    me = me_ref[0]
    partner = jnp.bitwise_xor(me, 1)
    own_home = jnp.clip(home_ref[me], 1, slots)
    far_home = jnp.clip(home_ref[partner], 1, slots)
    own_blocks = lax.shift_right_arithmetic(len_ref[me] + (CB - 1), 7)
    far_blocks = lax.shift_right_arithmetic(len_ref[partner] + (CB - 1), 7)
    own_tail = jnp.minimum(len_ref[me] - (own_home - 1) * CB, CB)
    far_tail = len_ref[partner] - (far_blocks - 1) * CB
    held = jnp.clip(far_blocks - far_home, 0, slots - own_home)
    away = jnp.clip(own_blocks - own_home, 0, slots - far_home)
    return own_home, own_tail, held, far_tail, away


def early_heads(away, heads, slots, fresh):
    result = jnp.int32(0)
    for count in range(1, slots):
        share = min(heads, int(round(count * heads / (slots + fresh))))
        result = jnp.where(away == count, share, result)
    return result


def total_of(refs, row):
    total = refs[0][row : row + 1, :]
    for ref in refs[1:]:
        total = total + ref[row : row + 1, :]
    return total


def lanes(head):
    return pl.ds(pl.multiple_of(head * HD, HD), HD)


class Stage:
    def __init__(self, q, q_scale, q_gain, keys, values, tail, fresh, out, stat, scratch):
        self.q, self.q_scale, self.q_gain = q, q_scale, q_gain
        self.keys, self.values, self.tail, self.fresh = keys, values, tail, fresh
        self.out, self.stat = out, stat
        self.scores, self.tops, self.weights = scratch
        self.rows = q.shape[0] // 2
        self.cached = keys.shape[0]
        self.total = self.cached + (fresh[0].shape[0] if fresh else 0)
        self.lane = lax.broadcasted_iota(jnp.int32, (self.rows, HD), 1)

    def piece(self, half):
        return pl.ds(half * self.rows, self.rows)

    def score(self, head, half):
        cut, piece = lanes(head), self.piece(half)
        raw = self.q[piece, cut].astype(jnp.float32)
        queries = (raw * self.q_scale[piece, :] * self.q_gain[:, cut]).astype(jnp.bfloat16)
        keys = self.keys[:, cut]
        if self.fresh:
            new_k, _, k_scale, k_gain = self.fresh
            raw_k = new_k[:, cut].astype(jnp.float32)
            keys = jnp.concatenate([keys, (raw_k * k_scale[...] * k_gain[:, cut]).astype(jnp.bfloat16)], axis=0)
        scores = lax.dot_general(queries, keys, (((1,), (1,)), ((), ())), preferred_element_type=jnp.float32)
        top = None
        for start in range(0, self.total, CB):
            column = scores[:, start : start + CB]
            if start == self.cached - CB:
                column = jnp.where(self.lane < self.tail, column, NEGATIVE)
            self.scores[half][:, start : start + CB] = column
            top = column if top is None else jnp.maximum(top, column)
        top = jnp.broadcast_to(jnp.max(top, axis=1, keepdims=True), (self.rows, HD))
        self.tops[half][...] = top

    def soften(self, head, half):
        top = self.tops[half][...]
        for start in range(0, self.total, CB):
            column = self.scores[half][:, start : start + CB]
            self.weights[half][:, start : start + CB] = jnp.exp2(column - top).astype(jnp.bfloat16)
        pltpu.store(self.stat.at[self.piece(half), :], top, mask=self.lane == head)

    def mix(self, head, slot, lane, half):
        cut = lanes(head)
        values = self.values[:, cut]
        if self.fresh:
            values = jnp.concatenate([values, self.fresh[1][:, cut]], axis=0)
        wide = jnp.concatenate([values, jnp.ones_like(values)], axis=1)
        mixture = jnp.dot(self.weights[half][:, : self.total], wide, preferred_element_type=jnp.float32)
        totals = mixture[:, HD:]
        inverse = pl.reciprocal(totals, approx=True)
        inverse = inverse * (2.0 - totals * inverse)
        self.out[self.piece(half), lanes(slot)] = (mixture[:, :HD] * inverse).astype(jnp.bfloat16)
        pltpu.store(self.stat.at[self.piece(half), :], totals, mask=self.lane == lane + SUM_LANE)

    def run(self, first, last, spare, ready, done):
        ready(first, True)
        self.score(first, 0)

        def step(head, carry):
            later = jnp.minimum(head + 1, last - 1)
            begun = head > first
            before = jnp.maximum(head - 1, first)
            ready(head + 1, False)
            self.score(head, 1)
            self.soften(head, 0)
            self.mix(before, jnp.where(begun, before, spare), jnp.where(begun, before, SUM_LANE - 1), 1)
            self.score(later, 0)
            self.soften(head, 1)
            self.mix(head, head, head, 0)

            @pl.when(begun)
            def _():
                done(before).start()

            return carry

        lax.fori_loop(first, last, step, 0)
        self.mix(last - 1, last - 1, last - 1, 1)
        done(last - 1).start()
        lax.fori_loop(first, last, lambda head, carry: (done(head).wait(), carry)[1], 0)


def loads(arrays, chunk, heads, sems):
    width = chunk * HD

    def copies(part):
        cut = pl.ds(pl.multiple_of(part * width, width), width)
        result = []
        for index, (source, target, rows) in enumerate(arrays):
            left = source.at[:, cut] if rows is None else source.at[rows, cut]
            right = target.at[:, cut] if rows is None else target.at[pl.ds(0, rows.size), cut]
            result.append(pltpu.make_async_copy(left, right, sems.at[index, part]))
        return result

    def start(first, last):
        def one(part, carry):
            for copy in copies(part):
                copy.start()
            return carry

        lax.fori_loop(first // chunk, (last + chunk - 1) // chunk, one, 0)

    def ready(first, last):
        def wait(head, at_start):
            if at_start:
                wanted = True
            else:
                wanted = (head < last) & (lax.rem(head, chunk) == 0)

            @pl.when(wanted)
            def _():
                for copy in copies(head // chunk):
                    copy.wait()

        return wait

    return start, ready


def early_kernel(me_ref, len_ref, home_ref, *refs, slots, heads, chunk, sums):
    own_squares, far_squares, refs = refs[:sums], refs[sums : 2 * sums], refs[2 * sums :]
    (q_any, far_q_any, k_any, v_any, nk_any, nv_any, qg, kg, far_any, far_stat_any, own_any, stat_any) = refs[:12]
    q, k, v, nk, nv, out, stat, q_scale, k_scale, s0, s1, t0, t1, w0, w1, in_sems, out_sems, stat_sem = refs[12:]
    own_home, own_tail, held, far_tail, away = counts(me_ref, len_ref, home_ref, slots)
    fresh_rows = nk.shape[0]
    scratch = ((s0, s1), (t0, t1), (w0, w1))

    def writer(target):
        def copy(head):
            return pltpu.make_async_copy(out.at[:, lanes(head)], target.at[:, lanes(head)], out_sems.at[head])

        return copy

    def write_stat(target):
        copy = pltpu.make_async_copy(stat, target, stat_sem)
        copy.start()
        copy.wait()

    for count in range(1, slots):

        @pl.when(held == count)
        def _():
            size = count * CB
            rows = pl.ds(pl.multiple_of(jnp.minimum(own_home, slots - count) * CB, CB), size)
            start, ready = loads([(far_q_any, q, None), (k_any, k, rows), (v_any, v, rows)], chunk, heads, in_sems)
            start(0, heads)
            q_scale[...] = row_scale(total_of(far_squares, 0), HEADS * HD, SCALE)
            Stage(
                q, q_scale, qg, k.at[pl.ds(0, size), :], v.at[pl.ds(0, size), :], far_tail, None, out, stat, scratch
            ).run(0, heads, heads, ready(0, heads), writer(far_any))
            write_stat(far_stat_any)

    last = early_heads(away, heads, slots, fresh_rows // CB)

    @pl.when(last > 0)
    def _():
        start, ready = loads(
            [(q_any, q, None), (k_any, k, None), (v_any, v, None), (nk_any, nk, None), (nv_any, nv, None)],
            chunk, heads, in_sems,
        )
        start(0, last)
        q_scale[...] = row_scale(total_of(own_squares, 0), HEADS * HD, SCALE)
        k_scale[...] = row_scale(total_of(own_squares, 1), HEADS * HD, 1.0)
        Stage(q, q_scale, qg, k, v, own_tail, (nk, nv, k_scale, kg), out, stat, scratch).run(
            0, last, heads, ready(0, last), writer(own_any)
        )
        write_stat(stat_any)


def late_kernel(me_ref, len_ref, home_ref, *refs, slots, heads, chunk, sums):
    own_squares, refs = refs[:sums], refs[sums:]
    (q_any, k_any, v_any, nk_any, nv_any, qg, kg, _, _, own_any, stat_any) = refs[:11]
    q, k, v, nk, nv, out, stat, q_scale, k_scale, s0, s1, t0, t1, w0, w1, in_sems, out_sems, stat_sem = refs[11:]
    own_home, own_tail, held, far_tail, away = counts(me_ref, len_ref, home_ref, slots)
    fresh_rows = nk.shape[0]
    scratch = ((s0, s1), (t0, t1), (w0, w1))
    first = early_heads(away, heads, slots, fresh_rows // CB)

    def writer(head):
        return pltpu.make_async_copy(out.at[:, lanes(head)], own_any.at[:, lanes(head)], out_sems.at[head])

    for count in range(1, slots + 1):

        @pl.when((own_home == count) & (first < heads))
        def _():
            rows = pl.ds(0, count * CB)
            start, ready = loads(
                [(q_any, q, None), (k_any, k, rows), (v_any, v, rows), (nk_any, nk, None), (nv_any, nv, None)],
                chunk, heads, in_sems,
            )
            start(first, heads)

            @pl.when(first > 0)
            def _():
                copy = pltpu.make_async_copy(stat_any, stat, stat_sem)
                copy.start()
                copy.wait()

            q_scale[...] = row_scale(total_of(own_squares, 0), HEADS * HD, SCALE)
            k_scale[...] = row_scale(total_of(own_squares, 1), HEADS * HD, 1.0)
            Stage(
                q, q_scale, qg, k.at[rows, :], v.at[rows, :], own_tail, (nk, nv, k_scale, kg), out, stat, scratch
            ).run(first, heads, heads, ready(first, heads), writer)

            @pl.when(away > 0)
            def _():
                copy = pltpu.make_async_copy(stat, stat_any, stat_sem)
                copy.start()
                copy.wait()


def join_kernel(
    me_ref, len_ref, home_ref, own_any, stat_any, far_any, far_stat_any, out_any,
    own, far, stat, far_stat, in_sems, out_sems, *, slots, step_rows
):
    away = counts(me_ref, len_ref, home_ref, slots)[4]
    row_count = own.shape[0]
    steps = row_count // step_rows

    @pl.when(away > 0)
    def _():
        def piece(step):
            return pl.ds(pl.multiple_of(step * step_rows, step_rows), step_rows)

        def copies(step):
            rows = piece(step)
            pairs = ((own_any, own), (far_any, far), (stat_any, stat), (far_stat_any, far_stat))
            return [
                pltpu.make_async_copy(a.at[rows, :], b.at[rows, :], in_sems.at[i, step]) for i, (a, b) in enumerate(pairs)
            ]

        def write(step):
            return pltpu.make_async_copy(own.at[piece(step), :], out_any.at[piece(step), :], out_sems.at[step])

        for step in range(steps):
            for copy in copies(step):
                copy.start()

        def one(step, carry):
            for copy in copies(step):
                copy.wait()
            rows = piece(step)
            near, away_stat = stat[rows, :], far_stat[rows, :]
            top = jnp.maximum(near, away_stat)
            own_part = pltpu.roll(near, HD - SUM_LANE, 1) * jnp.exp2(near - top)
            far_part = pltpu.roll(away_stat, HD - SUM_LANE, 1) * jnp.exp2(away_stat - top)
            share = far_part / (own_part + far_part)
            for head in range(own.shape[1] // HD):
                cut = slice(head * HD, (head + 1) * HD)
                here = own[rows, cut].astype(jnp.float32)
                there = far[rows, cut].astype(jnp.float32)
                own[rows, cut] = (here + share[:, head : head + 1] * (there - here)).astype(jnp.bfloat16)
            write(step).start()
            return carry

        lax.fori_loop(0, steps, one, 0)
        for step in range(steps):
            write(step).wait()


def body(groups, tensors, new_q, new_k, new_v, cache_k, cache_v, q_gain, k_gain, cache_len, home_blocks):
    row_count, feature_count = new_q.shape
    heads = feature_count // HD
    slot_rows = cache_k.shape[0]
    slots = slot_rows // CB
    chunk = 2 if heads % 2 == 0 else 1
    half, keys = row_count // 2, slot_rows + row_count

    far_q = lax.ppermute(new_q, "group", swap_pairs(groups))
    wide_q = new_q.astype(jnp.float32)
    wide_k = new_k.astype(jnp.float32)
    squares = jnp.stack([jnp.sum(wide_q * wide_q, axis=1), jnp.sum(wide_k * wide_k, axis=1)])
    if tensors == 2:
        diagonal = [(source, source ^ 3) for source in range(groups * tensors)]
        own_squares = [squares, lax.ppermute(squares, "tensor", swap_pairs(tensors))]
        far_squares = [
            lax.ppermute(squares, "group", swap_pairs(groups)),
            lax.ppermute(squares, ("group", "tensor"), diagonal),
        ]
    else:
        own_squares = [lax.psum(squares, "tensor")]
        far_squares = [lax.ppermute(own_squares[0], "group", swap_pairs(groups))]
    sums = len(own_squares)

    me = lax.axis_index("group").astype(jnp.int32).reshape(1)
    q_gain = q_gain.reshape(1, feature_count)
    k_gain = k_gain.reshape(1, feature_count)
    scalars = (me, cache_len, home_blocks)
    smem = [pl.BlockSpec(memory_space=pltpu.SMEM)] * 3
    vmem = pl.BlockSpec(memory_space=pltpu.VMEM)
    anywhere = pl.BlockSpec(memory_space=pl.ANY)

    stat = jax.ShapeDtypeStruct((row_count, HD), jnp.float32)
    result = jax.ShapeDtypeStruct((row_count, feature_count), jnp.bfloat16)
    new_rows = pltpu.VMEM((row_count, feature_count), jnp.bfloat16)
    slot_space = pltpu.VMEM((slot_rows, feature_count), jnp.bfloat16)
    stat_space = pltpu.VMEM((row_count, HD), jnp.float32)
    space = [
        new_rows, slot_space, slot_space, new_rows, new_rows,
        pltpu.VMEM((row_count, feature_count + HD), jnp.bfloat16),
        stat_space, stat_space, stat_space,
        pltpu.VMEM((half, keys), jnp.float32), pltpu.VMEM((half, keys), jnp.float32),
        pltpu.VMEM((half, HD), jnp.float32), pltpu.VMEM((half, HD), jnp.float32),
        pltpu.VMEM((half, keys), jnp.bfloat16), pltpu.VMEM((half, keys), jnp.bfloat16),
        pltpu.SemaphoreType.DMA((5, heads // chunk)), pltpu.SemaphoreType.DMA((heads,)), pltpu.SemaphoreType.DMA,
    ]
    pairs = row_count * heads * CB

    def cost(blocks):
        return pl.CostEstimate(
            flops=4 * pairs * HD * blocks, bytes_accessed=4 * blocks * CB * feature_count, transcendentals=pairs * blocks
        )

    def params(size):
        return pltpu.CompilerParams(vmem_limit_bytes=size)

    far_out, far_stat, own_out, own_stat = pl.pallas_call(
        functools.partial(early_kernel, slots=slots, heads=heads, chunk=chunk, sums=sums),
        out_shape=(result, stat, result, stat),
        in_specs=smem + [vmem] * (2 * sums) + [anywhere] * 6 + [vmem] * 2,
        out_specs=(anywhere,) * 4,
        scratch_shapes=space,
        compiler_params=params(VMEM),
        cost_estimate=cost(6),
        name="early_attention",
    )(*scalars, *own_squares, *far_squares, new_q, far_q, cache_k, cache_v, new_k, new_v, q_gain, k_gain)
    back_out, back_stat = lax.ppermute((far_out, far_stat), "group", swap_pairs(groups))

    own_out, own_stat = pl.pallas_call(
        functools.partial(late_kernel, slots=slots, heads=heads, chunk=chunk, sums=sums),
        out_shape=(result, stat),
        in_specs=smem + [vmem] * sums + [anywhere] * 5 + [vmem] * 2 + [anywhere] * 2,
        out_specs=(anywhere,) * 2,
        scratch_shapes=space,
        input_output_aliases={10 + sums: 0, 11 + sums: 1},
        compiler_params=params(VMEM),
        cost_estimate=cost(6),
        name="late_attention",
    )(*scalars, *own_squares, new_q, cache_k, cache_v, new_k, new_v, q_gain, k_gain, own_out, own_stat)

    step_rows = 64
    steps = row_count // step_rows
    return pl.pallas_call(
        functools.partial(join_kernel, slots=slots, step_rows=step_rows),
        out_shape=result,
        in_specs=smem + [anywhere] * 4,
        out_specs=anywhere,
        scratch_shapes=[
            new_rows, new_rows, stat_space, stat_space,
            pltpu.SemaphoreType.DMA((4, steps)), pltpu.SemaphoreType.DMA((steps,)),
        ],
        input_output_aliases={3: 0},
        compiler_params=params(16 * 1024 * 1024),
        name="join_parts",
    )(*scalars, own_out, own_stat, back_out, back_stat)


def solution(mesh):
    placed = (
        P("group", "tensor"),
        P("group", "tensor"),
        P("group", "tensor"),
        P("group", "tensor"),
        P("group", "tensor"),
        P("tensor"),
        P("tensor"),
        P(),
        P(),
    )
    return jax.shard_map(
        functools.partial(body, mesh.shape["group"], mesh.shape["tensor"]),
        mesh=mesh,
        in_specs=placed,
        out_specs=P("group", "tensor"),
        check_vma=False,
    )
```

```python
import functools
import math

import jax
import jax.numpy as jnp
from jax import lax
from jax.experimental import pallas as pl
from jax.experimental.pallas import tpu as pltpu
from jax.sharding import PartitionSpec as P

HEADS = 40
HD = 128
CB = 128
EPS = 1e-06
NEGATIVE = -1e30
SCALE = math.log2(math.e) / math.sqrt(HD)
SUM_LANE = 64
VMEM = 48 * 1024 * 1024
KEYS = 256


def swap_pairs(count):
    return [(source, source ^ 1) for source in range(count)]


def row_scale(square, width, factor):
    scale = lax.rsqrt(square / width + EPS) * factor
    pieces = []
    for start in range(0, square.shape[1], HD):
        piece = jnp.broadcast_to(scale[:, start : start + HD], (HD, HD))
        pieces.append(jnp.transpose(piece))
    return jnp.concatenate(pieces, axis=0)


def counts(me_ref, len_ref, home_ref, slots):
    me = me_ref[0]
    partner = jnp.bitwise_xor(me, 1)
    own_home = jnp.clip(home_ref[me], 1, slots)
    far_home = jnp.clip(home_ref[partner], 1, slots)
    own_blocks = lax.shift_right_arithmetic(len_ref[me] + (CB - 1), 7)
    far_blocks = lax.shift_right_arithmetic(len_ref[partner] + (CB - 1), 7)
    own_tail = jnp.minimum(len_ref[me] - (own_home - 1) * CB, CB)
    far_tail = len_ref[partner] - (far_blocks - 1) * CB
    held = jnp.clip(far_blocks - far_home, 0, slots - own_home)
    away = jnp.clip(own_blocks - own_home, 0, slots - far_home)
    return own_home, own_tail, held, far_tail, away


def early_heads(away, heads, slots, fresh):
    result = jnp.int32(0)
    for count in range(1, slots):
        share = min(heads, 2 * int(round(count * heads / (slots + fresh) / 2)))
        result = jnp.where(away == count, share, result)
    return result


def total_of(refs, row):
    total = refs[0][row : row + 1, :]
    for ref in refs[1:]:
        total = total + ref[row : row + 1, :]
    return total


def lanes(head):
    return pl.ds(pl.multiple_of(head * HD, HD), HD)


class Stage:
    def __init__(self, q, q_scale, q_gain, keys, values, tail, fresh, out, stat, scratch):
        self.q, self.q_scale, self.q_gain = q, q_scale, q_gain
        self.keys, self.values, self.tail, self.fresh = keys, values, tail, fresh
        self.out, self.stat = out, stat
        self.scores, self.tops, self.weights = scratch
        self.rows = q.shape[0]
        self.cached = keys.shape[0]
        self.total = self.cached + (fresh[0].shape[0] if fresh else 0)
        self.lane = lax.broadcasted_iota(jnp.int32, (self.rows, HD), 1)

    def score(self, head, slot):
        cut = lanes(head)
        raw = self.q[:, cut].astype(jnp.float32)
        queries = (raw * self.q_scale[...] * self.q_gain[:, cut]).astype(jnp.bfloat16)
        keys = self.keys[:, cut]
        if self.fresh:
            new_k, _, k_scale, k_gain = self.fresh
            raw_k = new_k[:, cut].astype(jnp.float32)
            keys = jnp.concatenate([keys, (raw_k * k_scale[...] * k_gain[:, cut]).astype(jnp.bfloat16)], axis=0)
        top = None
        for begin in range(0, self.total, KEYS):
            scores = lax.dot_general(
                queries, keys[begin : begin + KEYS], (((1,), (1,)), ((), ())), preferred_element_type=jnp.float32
            )
            for start in range(begin, min(begin + KEYS, self.total), CB):
                column = scores[:, start - begin : start - begin + CB]
                if start == self.cached - CB:
                    column = jnp.where(self.lane < self.tail, column, NEGATIVE)
                self.scores[slot][:, start : start + CB] = column
                top = column if top is None else jnp.maximum(top, column)
        self.tops[slot][...] = jnp.broadcast_to(jnp.max(top, axis=1, keepdims=True), (self.rows, HD))

    def soften(self, head, slot):
        top = self.tops[slot][...]
        for start in range(0, self.total, CB):
            column = self.scores[slot][:, start : start + CB]
            self.weights[slot][:, start : start + CB] = jnp.exp2(column - top).astype(jnp.bfloat16)
        pltpu.store(self.stat, top, mask=self.lane == head)

    def mix(self, head, target, lane, slot):
        cut = lanes(head)
        values = self.values[:, cut]
        if self.fresh:
            values = jnp.concatenate([values, self.fresh[1][:, cut]], axis=0)
        wide = jnp.concatenate([values, jnp.ones_like(values)], axis=1)
        mixture = jnp.dot(self.weights[slot][:, : self.total], wide, preferred_element_type=jnp.float32)
        totals = mixture[:, HD:]
        inverse = pl.reciprocal(totals, approx=True)
        inverse = inverse * (2.0 - totals * inverse)
        self.out[:, lanes(target)] = (mixture[:, :HD] * inverse).astype(jnp.bfloat16)
        pltpu.store(self.stat, totals, mask=self.lane == lane + SUM_LANE)

    def run(self, first, last, spare, ready, done, finish=None):
        ready(first, True)
        self.score(first, 0)
        count = last - first
        paired = lax.rem(count, 2) == 0

        def step(index, carry):
            head = first + 2 * index
            second = jnp.minimum(head + 1, last - 1)
            later = jnp.minimum(head + 2, last - 1)
            begun = index > 0
            before = jnp.maximum(head - 1, first)
            ready(head + 1, False)
            ready(head + 2, False)
            self.score(second, 1)
            self.soften(head, 0)
            self.mix(before, jnp.where(begun, before, spare), jnp.where(begun, before, SUM_LANE - 1), 1)
            self.score(later, 0)
            self.soften(second, 1)
            self.mix(head, head, head, 0)
            done(head).start()

            @pl.when(begun)
            def _():
                done(before).start()

            return carry

        lax.fori_loop(0, lax.shift_right_logical(count + 1, 1), step, 0)
        self.mix(last - 1, jnp.where(paired, last - 1, spare), last - 1, 1)

        @pl.when(paired)
        def _():
            done(last - 1).start()

        if finish is not None:
            finish()
        lax.fori_loop(first, last, lambda head, carry: (done(head).wait(), carry)[1], 0)


def loads(arrays, chunk, heads, sems):
    width = chunk * HD

    def copies(part):
        cut = pl.ds(pl.multiple_of(part * width, width), width)
        result = []
        for index, (source, target, rows) in enumerate(arrays):
            left = source.at[:, cut] if rows is None else source.at[rows, cut]
            right = target.at[:, cut] if rows is None else target.at[pl.ds(0, rows.size), cut]
            result.append(pltpu.make_async_copy(left, right, sems.at[index, part]))
        return result

    def start(first, last, between):
        def one(part, carry):
            for copy in copies(part):
                copy.start()
            return carry

        one(first // chunk, 0)
        between()
        lax.fori_loop(first // chunk + 1, (last + chunk - 1) // chunk, one, 0)

    def ready(first, last):
        def wait(head, at_start):
            if at_start:
                wanted = True
            else:
                wanted = (head < last) & (lax.rem(head, chunk) == 0)

            @pl.when(wanted)
            def _():
                for copy in copies(head // chunk):
                    copy.wait()

        return wait

    return start, ready


def early_kernel(me_ref, len_ref, home_ref, *refs, slots, heads, chunk, sums):
    own_squares, far_squares, refs = refs[:sums], refs[sums : 2 * sums], refs[2 * sums :]
    (q_any, far_q_any, k_any, v_any, nk_any, nv_any, qg, kg, far_any, far_stat_any, own_any, stat_any) = refs[:12]
    q, k, v, nk, nv, out, stat, q_scale, k_scale, s0, s1, t0, t1, w0, w1, in_sems, out_sems, stat_sem = refs[12:]
    own_home, own_tail, held, far_tail, away = counts(me_ref, len_ref, home_ref, slots)
    fresh_rows = nk.shape[0]
    scratch = ((s0, s1), (t0, t1), (w0, w1))

    def writer(target):
        def copy(head):
            return pltpu.make_async_copy(out.at[:, lanes(head)], target.at[:, lanes(head)], out_sems.at[head])

        return copy

    def write_stat(target):
        return pltpu.make_async_copy(stat, target, stat_sem)

    def far_scale():
        q_scale[...] = row_scale(total_of(far_squares, 0), HEADS * HD, SCALE)

    def own_scale():
        q_scale[...] = row_scale(total_of(own_squares, 0), HEADS * HD, SCALE)
        k_scale[...] = row_scale(total_of(own_squares, 1), HEADS * HD, 1.0)

    for count in range(1, slots):

        @pl.when(held == count)
        def _():
            size = count * CB
            rows = pl.ds(pl.multiple_of(jnp.minimum(own_home, slots - count) * CB, CB), size)
            start, ready = loads([(far_q_any, q, None), (k_any, k, rows), (v_any, v, rows)], chunk, heads, in_sems)
            start(0, heads, far_scale)
            Stage(
                q, q_scale, qg, k.at[pl.ds(0, size), :], v.at[pl.ds(0, size), :], far_tail, None, out, stat, scratch
            ).run(0, heads, heads, ready(0, heads), writer(far_any), write_stat(far_stat_any).start)
            write_stat(far_stat_any).wait()

    last = early_heads(away, heads, slots, fresh_rows // CB)

    @pl.when(last > 0)
    def _():
        start, ready = loads(
            [(q_any, q, None), (k_any, k, None), (v_any, v, None), (nk_any, nk, None), (nv_any, nv, None)],
            chunk, heads, in_sems,
        )
        start(0, last, own_scale)
        Stage(q, q_scale, qg, k, v, own_tail, (nk, nv, k_scale, kg), out, stat, scratch).run(
            0, last, heads, ready(0, last), writer(own_any), write_stat(stat_any).start
        )
        write_stat(stat_any).wait()


def late_kernel(me_ref, len_ref, home_ref, *refs, slots, heads, chunk, sums):
    own_squares, refs = refs[:sums], refs[sums:]
    (q_any, k_any, v_any, nk_any, nv_any, qg, kg, _, _, own_any, stat_any) = refs[:11]
    q, k, v, nk, nv, out, stat, q_scale, k_scale, s0, s1, t0, t1, w0, w1, in_sems, out_sems, stat_sem = refs[11:]
    own_home, own_tail, held, far_tail, away = counts(me_ref, len_ref, home_ref, slots)
    fresh_rows = nk.shape[0]
    scratch = ((s0, s1), (t0, t1), (w0, w1))
    first = early_heads(away, heads, slots, fresh_rows // CB)

    def own_scale():
        q_scale[...] = row_scale(total_of(own_squares, 0), HEADS * HD, SCALE)
        k_scale[...] = row_scale(total_of(own_squares, 1), HEADS * HD, 1.0)

    def writer(head):
        return pltpu.make_async_copy(out.at[:, lanes(head)], own_any.at[:, lanes(head)], out_sems.at[head])

    for count in range(1, slots + 1):

        @pl.when((own_home == count) & (first < heads))
        def _():
            rows = pl.ds(0, count * CB)
            start, ready = loads(
                [(q_any, q, None), (k_any, k, rows), (v_any, v, rows), (nk_any, nk, None), (nv_any, nv, None)],
                chunk, heads, in_sems,
            )
            start(first, heads, own_scale)

            @pl.when(first > 0)
            def _():
                copy = pltpu.make_async_copy(stat_any, stat, stat_sem)
                copy.start()
                copy.wait()

            Stage(
                q, q_scale, qg, k.at[rows, :], v.at[rows, :], own_tail, (nk, nv, k_scale, kg), out, stat, scratch
            ).run(first, heads, heads, ready(first, heads), writer)

            @pl.when(away > 0)
            def _():
                copy = pltpu.make_async_copy(stat, stat_any, stat_sem)
                copy.start()
                copy.wait()


def join_kernel(
    me_ref, len_ref, home_ref, own_any, stat_any, far_any, far_stat_any, out_any,
    own, far, stat, far_stat, in_sems, out_sems, *, slots, step_rows
):
    away = counts(me_ref, len_ref, home_ref, slots)[4]
    row_count = own.shape[0]
    steps = row_count // step_rows
    width = 2 * HD if own.shape[1] % (2 * HD) == 0 else HD

    @pl.when(away > 0)
    def _():
        def piece(step):
            return pl.ds(pl.multiple_of(step * step_rows, step_rows), step_rows)

        def copies(step):
            rows = piece(step)
            pairs = ((own_any, own), (far_any, far), (stat_any, stat), (far_stat_any, far_stat))
            return [
                pltpu.make_async_copy(a.at[rows, :], b.at[rows, :], in_sems.at[i, step]) for i, (a, b) in enumerate(pairs)
            ]

        def write(step):
            return pltpu.make_async_copy(own.at[piece(step), :], out_any.at[piece(step), :], out_sems.at[step])

        for step in range(steps):
            for copy in copies(step):
                copy.start()

        def one(step, carry):
            for copy in copies(step):
                copy.wait()
            rows = piece(step)
            near, away_stat = stat[rows, :], far_stat[rows, :]
            top = jnp.maximum(near, away_stat)
            own_part = pltpu.roll(near, HD - SUM_LANE, 1) * jnp.exp2(near - top)
            far_part = pltpu.roll(away_stat, HD - SUM_LANE, 1) * jnp.exp2(away_stat - top)
            known = lax.broadcasted_iota(jnp.int32, near.shape, 1) < own.shape[1] // HD
            share = jnp.where(known, far_part / (own_part + far_part), 0.0)
            high = share.astype(jnp.bfloat16)
            for begin in range(0, own.shape[1], width):
                cut = slice(begin, begin + width)
                lane = lax.broadcasted_iota(jnp.int32, (HD, width), 0)
                column = lax.broadcasted_iota(jnp.int32, (HD, width), 1)
                first = (lane - begin // HD) * HD
                spread = ((column >= first) & (column < first + HD)).astype(jnp.bfloat16)
                wide = jnp.dot(high, spread, preferred_element_type=jnp.float32)
                here = own[rows, cut].astype(jnp.float32)
                there = far[rows, cut].astype(jnp.float32)
                own[rows, cut] = (here + wide * (there - here)).astype(jnp.bfloat16)
            write(step).start()
            return carry

        lax.fori_loop(0, steps, one, 0)
        for step in range(steps):
            write(step).wait()


def body(groups, tensors, new_q, new_k, new_v, cache_k, cache_v, q_gain, k_gain, cache_len, home_blocks):
    row_count, feature_count = new_q.shape
    heads = feature_count // HD
    slot_rows = cache_k.shape[0]
    slots = slot_rows // CB
    chunk = 4 if heads % 4 == 0 else 1
    half, keys = row_count, slot_rows + row_count

    far_q = lax.ppermute(new_q, "group", swap_pairs(groups))
    wide_q = new_q.astype(jnp.float32)
    wide_k = new_k.astype(jnp.float32)
    squares = jnp.stack([jnp.sum(wide_q * wide_q, axis=1), jnp.sum(wide_k * wide_k, axis=1)])
    if tensors == 2:
        squares = squares + lax.ppermute(squares, "tensor", swap_pairs(tensors))
    else:
        squares = lax.psum(squares, "tensor")
    own_squares = [squares]
    far_squares = [lax.ppermute(squares, "group", swap_pairs(groups))]
    sums = len(own_squares)

    me = lax.axis_index("group").astype(jnp.int32).reshape(1)
    q_gain = q_gain.reshape(1, feature_count)
    k_gain = k_gain.reshape(1, feature_count)
    scalars = (me, cache_len, home_blocks)
    smem = [pl.BlockSpec(memory_space=pltpu.SMEM)] * 3
    vmem = pl.BlockSpec(memory_space=pltpu.VMEM)
    anywhere = pl.BlockSpec(memory_space=pl.ANY)
    distant = pl.BlockSpec(memory_space=pltpu.HBM)

    stat = jax.ShapeDtypeStruct((row_count, HD), jnp.float32)
    result = jax.ShapeDtypeStruct((row_count, feature_count), jnp.bfloat16)
    new_rows = pltpu.VMEM((row_count, feature_count), jnp.bfloat16)
    slot_space = pltpu.VMEM((slot_rows, feature_count), jnp.bfloat16)
    stat_space = pltpu.VMEM((row_count, HD), jnp.float32)
    space = [
        new_rows, slot_space, slot_space, new_rows, new_rows,
        pltpu.VMEM((row_count, feature_count + HD), jnp.bfloat16),
        stat_space, stat_space, stat_space,
        pltpu.VMEM((half, keys), jnp.float32), pltpu.VMEM((half, keys), jnp.float32),
        pltpu.VMEM((half, HD), jnp.float32), pltpu.VMEM((half, HD), jnp.float32),
        pltpu.VMEM((half, keys), jnp.bfloat16), pltpu.VMEM((half, keys), jnp.bfloat16),
        pltpu.SemaphoreType.DMA((5, heads // chunk)), pltpu.SemaphoreType.DMA((heads,)), pltpu.SemaphoreType.DMA,
    ]
    pairs = row_count * heads * CB

    def cost(blocks):
        return pl.CostEstimate(
            flops=4 * pairs * HD * blocks, bytes_accessed=4 * blocks * CB * feature_count, transcendentals=pairs * blocks
        )

    def params(size):
        return pltpu.CompilerParams(vmem_limit_bytes=size)

    far_out, far_stat, own_out, own_stat = pl.pallas_call(
        functools.partial(early_kernel, slots=slots, heads=heads, chunk=chunk, sums=sums),
        out_shape=(result, stat, result, stat),
        in_specs=smem + [vmem] * (2 * sums) + [distant, anywhere] + [distant] * 4 + [vmem] * 2,
        out_specs=(anywhere,) * 4,
        scratch_shapes=space,
        compiler_params=params(VMEM),
        cost_estimate=cost(6),
        name="early_attention",
    )(*scalars, *own_squares, *far_squares, new_q, far_q, cache_k, cache_v, new_k, new_v, q_gain, k_gain)
    back_out, back_stat = lax.ppermute((far_out, far_stat), "group", swap_pairs(groups))

    own_out, own_stat = pl.pallas_call(
        functools.partial(late_kernel, slots=slots, heads=heads, chunk=chunk, sums=sums),
        out_shape=(result, stat),
        in_specs=smem + [vmem] * sums + [distant] * 5 + [vmem] * 2 + [anywhere] * 2,
        out_specs=(anywhere,) * 2,
        scratch_shapes=space,
        input_output_aliases={10 + sums: 0, 11 + sums: 1},
        compiler_params=params(VMEM),
        cost_estimate=cost(6),
        name="late_attention",
    )(*scalars, *own_squares, new_q, cache_k, cache_v, new_k, new_v, q_gain, k_gain, own_out, own_stat)

    step_rows = 128
    steps = row_count // step_rows
    return pl.pallas_call(
        functools.partial(join_kernel, slots=slots, step_rows=step_rows),
        out_shape=result,
        in_specs=smem + [anywhere] * 4,
        out_specs=anywhere,
        scratch_shapes=[
            new_rows, new_rows, stat_space, stat_space,
            pltpu.SemaphoreType.DMA((4, steps)), pltpu.SemaphoreType.DMA((steps,)),
        ],
        input_output_aliases={3: 0},
        compiler_params=params(16 * 1024 * 1024),
        name="join_parts",
    )(*scalars, own_out, own_stat, back_out, back_stat)


def solution(mesh):
    placed = (
        P("group", "tensor"),
        P("group", "tensor"),
        P("group", "tensor"),
        P("group", "tensor"),
        P("group", "tensor"),
        P("tensor"),
        P("tensor"),
        P(),
        P(),
    )
    return jax.shard_map(
        functools.partial(body, mesh.shape["group"], mesh.shape["tensor"]),
        mesh=mesh,
        in_specs=placed,
        out_specs=P("group", "tensor"),
        check_vma=False,
    )
```

```python
import functools
import math

import jax
import jax.numpy as jnp
from jax import lax
from jax.experimental import pallas as pl
from jax.experimental.pallas import tpu as pltpu
from jax.sharding import PartitionSpec as P

HEADS = 40
HD = 128
CB = 128
EPS = 1e-06
NEGATIVE = -1e30
SCALE = math.log2(math.e) / math.sqrt(HD)
SUM_LANE = 64
VMEM = 53 * 1024 * 1024
KEYS = 256


def swap_pairs(count):
    return [(source, source ^ 1) for source in range(count)]


def row_scale(square, width, factor):
    scale = lax.rsqrt(square / width + EPS) * factor
    pieces = []
    for start in range(0, square.shape[1], HD):
        piece = jnp.broadcast_to(scale[:, start : start + HD], (HD, HD))
        pieces.append(jnp.transpose(piece))
    return jnp.concatenate(pieces, axis=0)


def counts(facts_ref, slots):
    requests = (facts_ref.shape[0] - 1) // 2
    me = facts_ref[0]
    partner = jnp.bitwise_xor(me, 1)
    own_length, far_length = facts_ref[1 + me], facts_ref[1 + partner]
    own_home = jnp.clip(facts_ref[1 + requests + me], 1, slots)
    far_home = jnp.clip(facts_ref[1 + requests + partner], 1, slots)
    own_blocks = lax.shift_right_arithmetic(own_length + (CB - 1), 7)
    far_blocks = lax.shift_right_arithmetic(far_length + (CB - 1), 7)
    own_tail = jnp.minimum(own_length - (own_home - 1) * CB, CB)
    far_tail = far_length - (far_blocks - 1) * CB
    held = jnp.clip(far_blocks - far_home, 0, slots - own_home)
    away = jnp.clip(own_blocks - own_home, 0, slots - far_home)
    return own_home, own_tail, held, far_tail, away


def early_heads(away, heads, slots, fresh):
    result = jnp.int32(0)
    for count in range(1, slots):
        share = min(heads, 2 * int(round(count * heads / (slots + fresh) / 2)))
        result = jnp.where(away == count, share, result)
    return result


def total_of(refs, row):
    total = refs[0][row : row + 1, :]
    for ref in refs[1:]:
        total = total + ref[row : row + 1, :]
    return total


def lanes(head):
    return pl.ds(pl.multiple_of(head * HD, HD), HD)


class Stage:
    def __init__(self, q, q_scale, q_gain, keys, values, tail, fresh, out, stat, scratch):
        self.q, self.q_scale, self.q_gain = q, q_scale, q_gain
        self.keys, self.values, self.tail, self.fresh = keys, values, tail, fresh
        self.out, self.stat = out, stat
        self.scores, self.tops, self.weights = scratch
        self.rows = q.shape[0]
        self.cached = keys.shape[0]
        self.total = self.cached + (fresh[0].shape[0] if fresh else 0)
        self.lane = lax.broadcasted_iota(jnp.int32, (self.rows, HD), 1)

    def score(self, head, slot):
        cut = lanes(head)
        raw = self.q[:, cut].astype(jnp.float32)
        queries = (raw * self.q_scale[...] * self.q_gain[:, cut]).astype(jnp.bfloat16)
        keys = self.keys[:, cut]
        if self.fresh:
            new_k, _, k_scale, k_gain = self.fresh
            raw_k = new_k[:, cut].astype(jnp.float32)
            keys = jnp.concatenate([keys, (raw_k * k_scale[...] * k_gain[:, cut]).astype(jnp.bfloat16)], axis=0)
        top = None
        for begin in range(0, self.total, KEYS):
            scores = lax.dot_general(
                queries, keys[begin : begin + KEYS], (((1,), (1,)), ((), ())), preferred_element_type=jnp.float32
            )
            for start in range(begin, min(begin + KEYS, self.total), CB):
                column = scores[:, start - begin : start - begin + CB]
                if start == self.cached - CB:
                    column = jnp.where(self.lane < self.tail, column, NEGATIVE)
                self.scores[slot][:, start : start + CB] = column
                top = column if top is None else jnp.maximum(top, column)
        self.tops[slot][...] = jnp.broadcast_to(jnp.max(top, axis=1, keepdims=True), (self.rows, HD))

    def soften(self, head, slot):
        top = self.tops[slot][...]
        for start in range(0, self.total, CB):
            column = self.scores[slot][:, start : start + CB]
            self.weights[slot][:, start : start + CB] = jnp.exp2(column - top).astype(jnp.bfloat16)
        pltpu.store(self.stat, top, mask=self.lane == head)

    def mix(self, head, target, lane, slot):
        cut = lanes(head)
        values = self.values[:, cut]
        if self.fresh:
            values = jnp.concatenate([values, self.fresh[1][:, cut]], axis=0)
        wide = jnp.concatenate([values, jnp.ones_like(values)], axis=1)
        mixture = jnp.dot(self.weights[slot][:, : self.total], wide, preferred_element_type=jnp.float32)
        totals = mixture[:, HD:]
        inverse = pl.reciprocal(totals, approx=True)
        inverse = inverse * (2.0 - totals * inverse)
        self.out[:, lanes(target)] = (mixture[:, :HD] * inverse).astype(jnp.bfloat16)
        pltpu.store(self.stat, totals, mask=self.lane == lane + SUM_LANE)

    def run(self, first, last, spare, ready, done, finish=None):
        ready(first, True)
        self.score(first, 0)
        count = last - first
        paired = lax.rem(count, 2) == 0

        def step(index, carry):
            head = first + 2 * index
            second = jnp.minimum(head + 1, last - 1)
            later = jnp.minimum(head + 2, last - 1)
            begun = index > 0
            before = jnp.maximum(head - 1, first)
            ready(head + 1, False)
            ready(head + 2, False)
            self.score(second, 1)
            self.soften(head, 0)
            self.mix(before, jnp.where(begun, before, spare), jnp.where(begun, before, SUM_LANE - 1), 1)
            self.score(later, 0)
            self.soften(second, 1)
            self.mix(head, head, head, 0)
            done(head).start()

            @pl.when(begun)
            def _():
                done(before).start()

            return carry

        lax.fori_loop(0, lax.shift_right_logical(count + 1, 1), step, 0)
        self.mix(last - 1, jnp.where(paired, last - 1, spare), last - 1, 1)

        @pl.when(paired)
        def _():
            done(last - 1).start()

        if finish is not None:
            finish()
        lax.fori_loop(first, last, lambda head, carry: (done(head).wait(), carry)[1], 0)


def loads(arrays, chunk, heads, sems):
    width = chunk * HD

    def copies(part):
        cut = pl.ds(pl.multiple_of(part * width, width), width)
        result = []
        for index, (source, target, rows) in enumerate(arrays):
            left = source.at[:, cut] if rows is None else source.at[rows, cut]
            right = target.at[:, cut] if rows is None else target.at[pl.ds(0, rows.size), cut]
            result.append(pltpu.make_async_copy(left, right, sems.at[index, part]))
        return result

    def start(first, last, between):
        def one(part, carry):
            for copy in copies(part):
                copy.start()
            return carry

        one(first // chunk, 0)
        between()
        lax.fori_loop(first // chunk + 1, (last + chunk - 1) // chunk, one, 0)

    def ready(first, last):
        def wait(head, at_start):
            if at_start:
                wanted = True
            else:
                wanted = (head < last) & (lax.rem(head, chunk) == 0)

            @pl.when(wanted)
            def _():
                for copy in copies(head // chunk):
                    copy.wait()

        return wait

    return start, ready


def early_kernel(facts_ref, *refs, slots, heads, chunk, sums):
    own_squares, far_squares, refs = refs[:sums], refs[sums : 2 * sums], refs[2 * sums :]
    (q_any, far_q_any, k_any, v_any, nk_any, nv_any, qg, kg, far_any, far_stat_any, own_any, stat_any) = refs[:12]
    q, k, v, nk, nv, out, stat, q_scale, k_scale, s0, s1, t0, t1, w0, w1, in_sems, out_sems, stat_sem = refs[12:]
    own_home, own_tail, held, far_tail, away = counts(facts_ref, slots)
    fresh_rows = nk.shape[0]
    scratch = ((s0, s1), (t0, t1), (w0, w1))

    def writer(target):
        def copy(head):
            return pltpu.make_async_copy(out.at[:, lanes(head)], target.at[:, lanes(head)], out_sems.at[head])

        return copy

    def write_stat(target):
        return pltpu.make_async_copy(stat, target, stat_sem)

    def far_scale():
        q_scale[...] = row_scale(total_of(far_squares, 0), HEADS * HD, SCALE)

    def own_scale():
        q_scale[...] = row_scale(total_of(own_squares, 0), HEADS * HD, SCALE)
        k_scale[...] = row_scale(total_of(own_squares, 1), HEADS * HD, 1.0)

    for count in range(1, slots):

        @pl.when(held == count)
        def _():
            size = count * CB
            rows = pl.ds(pl.multiple_of(jnp.minimum(own_home, slots - count) * CB, CB), size)
            start, ready = loads([(far_q_any, q, None), (k_any, k, rows), (v_any, v, rows)], chunk, heads, in_sems)
            start(0, heads, far_scale)
            Stage(
                q, q_scale, qg, k.at[pl.ds(0, size), :], v.at[pl.ds(0, size), :], far_tail, None, out, stat, scratch
            ).run(0, heads, heads, ready(0, heads), writer(far_any), write_stat(far_stat_any).start)
            write_stat(far_stat_any).wait()

    last = early_heads(away, heads, slots, fresh_rows // CB)

    @pl.when(last > 0)
    def _():
        start, ready = loads(
            [(q_any, q, None), (k_any, k, None), (v_any, v, None), (nk_any, nk, None), (nv_any, nv, None)],
            chunk, heads, in_sems,
        )
        start(0, last, own_scale)
        Stage(q, q_scale, qg, k, v, own_tail, (nk, nv, k_scale, kg), out, stat, scratch).run(
            0, last, heads, ready(0, last), writer(own_any), write_stat(stat_any).start
        )
        write_stat(stat_any).wait()


def late_kernel(facts_ref, *refs, slots, heads, chunk, sums):
    own_squares, refs = refs[:sums], refs[sums:]
    (q_any, k_any, v_any, nk_any, nv_any, qg, kg, _, _, own_any, stat_any) = refs[:11]
    q, k, v, nk, nv, out, stat, q_scale, k_scale, s0, s1, t0, t1, w0, w1, in_sems, out_sems, stat_sem = refs[11:]
    own_home, own_tail, held, far_tail, away = counts(facts_ref, slots)
    fresh_rows = nk.shape[0]
    scratch = ((s0, s1), (t0, t1), (w0, w1))
    first = early_heads(away, heads, slots, fresh_rows // CB)

    def own_scale():
        q_scale[...] = row_scale(total_of(own_squares, 0), HEADS * HD, SCALE)
        k_scale[...] = row_scale(total_of(own_squares, 1), HEADS * HD, 1.0)

    def writer(head):
        return pltpu.make_async_copy(out.at[:, lanes(head)], own_any.at[:, lanes(head)], out_sems.at[head])

    for count in range(1, slots + 1):

        @pl.when((own_home == count) & (first < heads))
        def _():
            rows = pl.ds(0, count * CB)
            start, ready = loads(
                [(q_any, q, None), (k_any, k, rows), (v_any, v, rows), (nk_any, nk, None), (nv_any, nv, None)],
                chunk, heads, in_sems,
            )
            start(first, heads, own_scale)

            @pl.when(first > 0)
            def _():
                copy = pltpu.make_async_copy(stat_any, stat, stat_sem)
                copy.start()
                copy.wait()

            Stage(
                q, q_scale, qg, k.at[rows, :], v.at[rows, :], own_tail, (nk, nv, k_scale, kg), out, stat, scratch
            ).run(first, heads, heads, ready(first, heads), writer)

            @pl.when(away > 0)
            def _():
                copy = pltpu.make_async_copy(stat, stat_any, stat_sem)
                copy.start()
                copy.wait()


def join_kernel(
    facts_ref, own_any, stat_any, far_any, far_stat_any, out_any,
    own, far, stat, far_stat, spread, out, in_sems, out_sems, *, slots, step_rows
):
    away = counts(facts_ref, slots)[4]
    row_count = own.shape[0]
    steps = row_count // step_rows

    @pl.when(away > 0)
    def _():
        def piece(step):
            return pl.ds(pl.multiple_of(step * step_rows, step_rows), step_rows)

        def copies(step):
            rows = piece(step)
            pairs = ((own_any, own), (far_any, far), (stat_any, stat), (far_stat_any, far_stat))
            return [
                pltpu.make_async_copy(a.at[rows, :], b.at[rows, :], in_sems.at[i, step]) for i, (a, b) in enumerate(pairs)
            ]

        def write(step):
            return pltpu.make_async_copy(out.at[piece(step), :], out_any.at[piece(step), :], out_sems.at[step])

        for step in range(steps):
            for copy in copies(step):
                copy.start()

        lane = lax.broadcasted_iota(jnp.int32, spread.shape, 0) * HD
        column = lax.broadcasted_iota(jnp.int32, spread.shape, 1)
        spread[...] = ((column >= lane) & (column < lane + HD)).astype(jnp.bfloat16)

        def one(step, carry):
            for copy in copies(step):
                copy.wait()
            rows = piece(step)
            near, away_stat = stat[rows, :], far_stat[rows, :]
            top = jnp.maximum(near, away_stat)
            own_part = pltpu.roll(near, HD - SUM_LANE, 1) * jnp.exp2(near - top)
            far_part = pltpu.roll(away_stat, HD - SUM_LANE, 1) * jnp.exp2(away_stat - top)
            known = lax.broadcasted_iota(jnp.int32, near.shape, 1) < own.shape[1] // HD
            share = jnp.where(known, far_part / (own_part + far_part), 0.0)
            wide = jnp.dot(share.astype(jnp.bfloat16), spread[...], preferred_element_type=jnp.float32)
            here = own[rows, :].astype(jnp.float32)
            there = far[rows, :].astype(jnp.float32)
            out[rows, :] = (here + wide * (there - here)).astype(jnp.bfloat16)
            write(step).start()
            return carry

        lax.fori_loop(0, steps, one, 0)
        for step in range(steps):
            write(step).wait()


def body(groups, tensors, new_q, new_k, new_v, cache_k, cache_v, q_gain, k_gain, cache_len, home_blocks):
    row_count, feature_count = new_q.shape
    heads = feature_count // HD
    slot_rows = cache_k.shape[0]
    slots = slot_rows // CB
    chunk = 2 if heads % 2 == 0 else 1
    half, keys = row_count, slot_rows + row_count

    far_q = lax.ppermute(new_q, "group", swap_pairs(groups))
    wide_q = new_q.astype(jnp.float32)
    wide_k = new_k.astype(jnp.float32)
    squares = jnp.stack([jnp.sum(wide_q * wide_q, axis=1), jnp.sum(wide_k * wide_k, axis=1)])
    if tensors == 2:
        squares = squares + lax.ppermute(squares, "tensor", swap_pairs(tensors))
    else:
        squares = lax.psum(squares, "tensor")
    own_squares = [squares]
    far_squares = [lax.ppermute(squares, "group", swap_pairs(groups))]
    sums = len(own_squares)

    me = lax.axis_index("group").astype(jnp.int32).reshape(1)
    q_gain = q_gain.reshape(1, feature_count)
    k_gain = k_gain.reshape(1, feature_count)
    facts = jnp.concatenate([me, cache_len, home_blocks])
    smem = [pl.BlockSpec(memory_space=pltpu.SMEM)]
    vmem = pl.BlockSpec(memory_space=pltpu.VMEM)
    anywhere = pl.BlockSpec(memory_space=pl.ANY)

    stat = jax.ShapeDtypeStruct((row_count, HD), jnp.float32)
    result = jax.ShapeDtypeStruct((row_count, feature_count), jnp.bfloat16)
    new_rows = pltpu.VMEM((row_count, feature_count), jnp.bfloat16)
    slot_space = pltpu.VMEM((slot_rows, feature_count), jnp.bfloat16)
    stat_space = pltpu.VMEM((row_count, HD), jnp.float32)
    space = [
        new_rows, slot_space, slot_space, new_rows, new_rows,
        pltpu.VMEM((row_count, feature_count + HD), jnp.bfloat16),
        stat_space, stat_space, stat_space,
        pltpu.VMEM((half, keys), jnp.float32), pltpu.VMEM((half, keys), jnp.float32),
        pltpu.VMEM((half, HD), jnp.float32), pltpu.VMEM((half, HD), jnp.float32),
        pltpu.VMEM((half, keys), jnp.bfloat16), pltpu.VMEM((half, keys), jnp.bfloat16),
        pltpu.SemaphoreType.DMA((5, heads // chunk)), pltpu.SemaphoreType.DMA((heads,)), pltpu.SemaphoreType.DMA,
    ]
    pairs = row_count * heads * CB

    def cost(blocks):
        return pl.CostEstimate(
            flops=4 * pairs * HD * blocks, bytes_accessed=4 * blocks * CB * feature_count, transcendentals=pairs * blocks
        )

    def params(size):
        return pltpu.CompilerParams(vmem_limit_bytes=size)

    far_out, far_stat, own_out, own_stat = pl.pallas_call(
        functools.partial(early_kernel, slots=slots, heads=heads, chunk=chunk, sums=sums),
        out_shape=(result, stat, result, stat),
        in_specs=smem + [vmem] * (2 * sums) + [anywhere] * 6 + [vmem] * 2,
        out_specs=(anywhere,) * 4,
        scratch_shapes=space,
        compiler_params=params(VMEM),
        cost_estimate=cost(6),
        name="early_attention",
    )(facts, *own_squares, *far_squares, new_q, far_q, cache_k, cache_v, new_k, new_v, q_gain, k_gain)
    back_out, back_stat = lax.ppermute((far_out, far_stat), "group", swap_pairs(groups))

    own_out, own_stat = pl.pallas_call(
        functools.partial(late_kernel, slots=slots, heads=heads, chunk=chunk, sums=sums),
        out_shape=(result, stat),
        in_specs=smem + [vmem] * sums + [anywhere] * 5 + [vmem] * 2 + [anywhere] * 2,
        out_specs=(anywhere,) * 2,
        scratch_shapes=space,
        input_output_aliases={8 + sums: 0, 9 + sums: 1},
        compiler_params=params(VMEM),
        cost_estimate=cost(6),
        name="late_attention",
    )(facts, *own_squares, new_q, cache_k, cache_v, new_k, new_v, q_gain, k_gain, own_out, own_stat)

    step_rows = 64
    steps = row_count // step_rows
    return pl.pallas_call(
        functools.partial(join_kernel, slots=slots, step_rows=step_rows),
        out_shape=result,
        in_specs=smem + [anywhere] * 4,
        out_specs=anywhere,
        scratch_shapes=[
            new_rows, new_rows, stat_space, stat_space,
            pltpu.VMEM((HD, feature_count), jnp.bfloat16), new_rows,
            pltpu.SemaphoreType.DMA((4, steps)), pltpu.SemaphoreType.DMA((steps,)),
        ],
        input_output_aliases={1: 0},
        compiler_params=params(24 * 1024 * 1024),
        name="join_parts",
    )(facts, own_out, own_stat, back_out, back_stat)


def solution(mesh):
    placed = (
        P("group", "tensor"),
        P("group", "tensor"),
        P("group", "tensor"),
        P("group", "tensor"),
        P("group", "tensor"),
        P("tensor"),
        P("tensor"),
        P(),
        P(),
    )
    return jax.shard_map(
        functools.partial(body, mesh.shape["group"], mesh.shape["tensor"]),
        mesh=mesh,
        in_specs=placed,
        out_specs=P("group", "tensor"),
        check_vma=False,
    )
```

```python
import functools
import math

import jax
import jax.numpy as jnp
from jax import lax
from jax.experimental import pallas as pl
from jax.experimental.pallas import tpu as pltpu
from jax.sharding import PartitionSpec as P

HEADS = 40
HD = 128
CB = 128
EPS = 1e-06
NEGATIVE = -1e30
SCALE = math.log2(math.e) / math.sqrt(HD)
SUM_LANE = 64
VMEM = 53 * 1024 * 1024
KEYS = 256


def swap_pairs(count):
    return [(source, source ^ 1) for source in range(count)]


def row_scale(square, width, factor):
    scale = lax.rsqrt(square / width + EPS) * factor
    pieces = []
    for start in range(0, square.shape[1], HD):
        piece = jnp.broadcast_to(scale[:, start : start + HD], (HD, HD))
        pieces.append(jnp.transpose(piece))
    return jnp.concatenate(pieces, axis=0)


def counts(facts_ref, slots):
    requests = (facts_ref.shape[0] - 1) // 2
    me = facts_ref[0]
    partner = jnp.bitwise_xor(me, 1)
    own_length, far_length = facts_ref[1 + me], facts_ref[1 + partner]
    own_home = jnp.clip(facts_ref[1 + requests + me], 1, slots)
    far_home = jnp.clip(facts_ref[1 + requests + partner], 1, slots)
    own_blocks = lax.shift_right_arithmetic(own_length + (CB - 1), 7)
    far_blocks = lax.shift_right_arithmetic(far_length + (CB - 1), 7)
    own_tail = jnp.minimum(own_length - (own_home - 1) * CB, CB)
    far_tail = far_length - (far_blocks - 1) * CB
    held = jnp.clip(far_blocks - far_home, 0, slots - own_home)
    away = jnp.clip(own_blocks - own_home, 0, slots - far_home)
    return own_home, own_tail, held, far_tail, away


def early_heads(away, heads, slots, fresh):
    result = jnp.int32(0)
    for count in range(1, slots):
        share = min(heads, 2 * math.ceil((2.25 + count) * heads / (slots + fresh + 2.25) / 2 - 0.05))
        result = jnp.where(away == count, share, result)
    return result


def total_of(refs, row):
    total = refs[0][row : row + 1, :]
    for ref in refs[1:]:
        total = total + ref[row : row + 1, :]
    return total


def lanes(head):
    return pl.ds(pl.multiple_of(head * HD, HD), HD)


class Stage:
    def __init__(self, q, q_scale, q_gain, keys, values, tail, fresh, out, stat, scratch):
        self.q, self.q_scale, self.q_gain = q, q_scale, q_gain
        self.keys, self.values, self.tail, self.fresh = keys, values, tail, fresh
        self.out, self.stat = out, stat
        self.scores, self.tops, self.weights = scratch
        self.rows = q.shape[0]
        self.cached = keys.shape[0]
        self.total = self.cached + (fresh[0].shape[0] if fresh else 0)
        self.lane = lax.broadcasted_iota(jnp.int32, (self.rows, HD), 1)

    def score(self, head, slot):
        cut = lanes(head)
        raw = self.q[:, cut].astype(jnp.float32)
        queries = (raw * self.q_scale[...] * self.q_gain[:, cut]).astype(jnp.bfloat16)
        keys = self.keys[:, cut]
        if self.fresh:
            new_k, _, k_scale, k_gain = self.fresh
            raw_k = new_k[:, cut].astype(jnp.float32)
            keys = jnp.concatenate([keys, (raw_k * k_scale[...] * k_gain[:, cut]).astype(jnp.bfloat16)], axis=0)
        top = None
        for begin in range(0, self.total, KEYS):
            scores = lax.dot_general(
                queries, keys[begin : begin + KEYS], (((1,), (1,)), ((), ())), preferred_element_type=jnp.float32
            )
            for start in range(begin, min(begin + KEYS, self.total), CB):
                column = scores[:, start - begin : start - begin + CB]
                if start == self.cached - CB:
                    column = jnp.where(self.lane < self.tail, column, NEGATIVE)
                self.scores[slot][:, start : start + CB] = column
                top = column if top is None else jnp.maximum(top, column)
        self.tops[slot][...] = jnp.broadcast_to(jnp.max(top, axis=1, keepdims=True), (self.rows, HD))

    def soften(self, head, slot):
        top = self.tops[slot][...]
        for start in range(0, self.total, CB):
            column = self.scores[slot][:, start : start + CB]
            self.weights[slot][:, start : start + CB] = jnp.exp2(column - top).astype(jnp.bfloat16)
        pltpu.store(self.stat, top, mask=self.lane == head)

    def mix(self, head, target, lane, slot):
        cut = lanes(head)
        values = self.values[:, cut]
        if self.fresh:
            values = jnp.concatenate([values, self.fresh[1][:, cut]], axis=0)
        wide = jnp.concatenate([values, jnp.ones_like(values)], axis=1)
        mixture = jnp.dot(self.weights[slot][:, : self.total], wide, preferred_element_type=jnp.float32)
        totals = mixture[:, HD:]
        inverse = pl.reciprocal(totals, approx=True)
        inverse = inverse * (2.0 - totals * inverse)
        self.out[:, lanes(target)] = (mixture[:, :HD] * inverse).astype(jnp.bfloat16)
        pltpu.store(self.stat, totals, mask=self.lane == lane + SUM_LANE)

    def run(self, first, last, spare, ready, done, finish=None):
        ready(first, True)
        self.score(first, 0)
        count = last - first
        paired = lax.rem(count, 2) == 0

        def step(index, carry):
            head = first + 2 * index
            second = jnp.minimum(head + 1, last - 1)
            later = jnp.minimum(head + 2, last - 1)
            begun = index > 0
            before = jnp.maximum(head - 1, first)
            ready(head + 1, False)
            ready(head + 2, False)
            self.score(second, 1)
            self.soften(head, 0)
            self.mix(before, jnp.where(begun, before, spare), jnp.where(begun, before, SUM_LANE - 1), 1)
            self.score(later, 0)
            self.soften(second, 1)
            self.mix(head, head, head, 0)
            done(head).start()

            @pl.when(begun)
            def _():
                done(before).start()

            return carry

        lax.fori_loop(0, lax.shift_right_logical(count + 1, 1), step, 0)
        self.mix(last - 1, jnp.where(paired, last - 1, spare), last - 1, 1)

        @pl.when(paired)
        def _():
            done(last - 1).start()

        if finish is not None:
            finish()
        lax.fori_loop(first, last, lambda head, carry: (done(head).wait(), carry)[1], 0)


def loads(arrays, chunk, heads, sems):
    width = chunk * HD

    def copies(part):
        cut = pl.ds(pl.multiple_of(part * width, width), width)
        result = []
        for index, (source, target, rows) in enumerate(arrays):
            left = source.at[:, cut] if rows is None else source.at[rows, cut]
            right = target.at[:, cut] if rows is None else target.at[pl.ds(0, rows.size), cut]
            result.append(pltpu.make_async_copy(left, right, sems.at[index, part]))
        return result

    def start(first, last, between):
        def one(part, carry):
            for copy in copies(part):
                copy.start()
            return carry

        one(first // chunk, 0)
        between()
        lax.fori_loop(first // chunk + 1, (last + chunk - 1) // chunk, one, 0)

    def ready(first, last):
        def wait(head, at_start):
            if at_start:
                wanted = True
            else:
                wanted = (head < last) & (lax.rem(head, chunk) == 0)

            @pl.when(wanted)
            def _():
                for copy in copies(head // chunk):
                    copy.wait()

        return wait

    return start, ready


def early_kernel(facts_ref, *refs, slots, heads, chunk, sums):
    own_squares, far_squares, refs = refs[:sums], refs[sums : 2 * sums], refs[2 * sums :]
    (q_any, far_q_any, k_any, v_any, nk_any, nv_any, qg, kg, far_any, far_stat_any, own_any, stat_any) = refs[:12]
    q, k, v, nk, nv, out, stat, q_scale, k_scale, s0, s1, t0, t1, w0, w1, in_sems, out_sems, stat_sem = refs[12:]
    own_home, own_tail, held, far_tail, away = counts(facts_ref, slots)
    fresh_rows = nk.shape[0]
    scratch = ((s0, s1), (t0, t1), (w0, w1))

    def writer(target):
        def copy(head):
            return pltpu.make_async_copy(out.at[:, lanes(head)], target.at[:, lanes(head)], out_sems.at[head])

        return copy

    def write_stat(target):
        return pltpu.make_async_copy(stat, target, stat_sem)

    def far_scale():
        q_scale[...] = row_scale(total_of(far_squares, 0), HEADS * HD, SCALE)

    def own_scale():
        q_scale[...] = row_scale(total_of(own_squares, 0), HEADS * HD, SCALE)
        k_scale[...] = row_scale(total_of(own_squares, 1), HEADS * HD, 1.0)

    for count in range(1, slots):

        @pl.when(held == count)
        def _():
            size = count * CB
            rows = pl.ds(pl.multiple_of(jnp.minimum(own_home, slots - count) * CB, CB), size)
            start, ready = loads([(far_q_any, q, None), (k_any, k, rows), (v_any, v, rows)], chunk, heads, in_sems)
            start(0, heads, far_scale)
            Stage(
                q, q_scale, qg, k.at[pl.ds(0, size), :], v.at[pl.ds(0, size), :], far_tail, None, out, stat, scratch
            ).run(0, heads, heads, ready(0, heads), writer(far_any), write_stat(far_stat_any).start)
            write_stat(far_stat_any).wait()

    last = early_heads(away, heads, slots, fresh_rows // CB)

    @pl.when(last > 0)
    def _():
        start, ready = loads(
            [(q_any, q, None), (k_any, k, None), (v_any, v, None), (nk_any, nk, None), (nv_any, nv, None)],
            chunk, heads, in_sems,
        )
        start(0, last, own_scale)
        Stage(q, q_scale, qg, k, v, own_tail, (nk, nv, k_scale, kg), out, stat, scratch).run(
            0, last, heads, ready(0, last), writer(own_any), write_stat(stat_any).start
        )
        write_stat(stat_any).wait()


def late_kernel(facts_ref, *refs, slots, heads, chunk, sums):
    own_squares, refs = refs[:sums], refs[sums:]
    (q_any, k_any, v_any, nk_any, nv_any, qg, kg, _, _, own_any, stat_any) = refs[:11]
    q, k, v, nk, nv, out, stat, q_scale, k_scale, s0, s1, t0, t1, w0, w1, in_sems, out_sems, stat_sem = refs[11:]
    own_home, own_tail, held, far_tail, away = counts(facts_ref, slots)
    fresh_rows = nk.shape[0]
    scratch = ((s0, s1), (t0, t1), (w0, w1))
    first = early_heads(away, heads, slots, fresh_rows // CB)

    def own_scale():
        q_scale[...] = row_scale(total_of(own_squares, 0), HEADS * HD, SCALE)
        k_scale[...] = row_scale(total_of(own_squares, 1), HEADS * HD, 1.0)

    def writer(head):
        return pltpu.make_async_copy(out.at[:, lanes(head)], own_any.at[:, lanes(head)], out_sems.at[head])

    for count in range(1, slots + 1):

        @pl.when((own_home == count) & (first < heads))
        def _():
            rows = pl.ds(0, count * CB)
            start, ready = loads(
                [(q_any, q, None), (k_any, k, rows), (v_any, v, rows), (nk_any, nk, None), (nv_any, nv, None)],
                chunk, heads, in_sems,
            )
            start(first, heads, own_scale)

            @pl.when(first > 0)
            def _():
                copy = pltpu.make_async_copy(stat_any, stat, stat_sem)
                copy.start()
                copy.wait()

            Stage(
                q, q_scale, qg, k.at[rows, :], v.at[rows, :], own_tail, (nk, nv, k_scale, kg), out, stat, scratch
            ).run(first, heads, heads, ready(first, heads), writer)

            @pl.when(away > 0)
            def _():
                copy = pltpu.make_async_copy(stat, stat_any, stat_sem)
                copy.start()
                copy.wait()


def join_kernel(facts_ref, own_any, stat, far, far_stat, out_any, own, out, in_sems, out_sems, *, slots, step_rows):
    away = counts(facts_ref, slots)[4]
    steps = own.shape[0] // step_rows

    @pl.when(away > 0)
    def _():
        def piece(step):
            return pl.ds(pl.multiple_of(step * step_rows, step_rows), step_rows)

        def read(step):
            return pltpu.make_async_copy(own_any.at[piece(step), :], own.at[piece(step), :], in_sems.at[step])

        def write(step):
            return pltpu.make_async_copy(out.at[piece(step), :], out_any.at[piece(step), :], out_sems.at[step])

        for step in range(steps):
            read(step).start()

        def one(step, carry):
            rows = piece(step)
            near, away_stat = stat[rows, :], far_stat[rows, :]
            top = jnp.maximum(near, away_stat)
            own_part = pltpu.roll(near, HD - SUM_LANE, 1) * jnp.exp2(near - top)
            far_part = pltpu.roll(away_stat, HD - SUM_LANE, 1) * jnp.exp2(away_stat - top)
            share = far_part / (own_part + far_part)
            read(step).wait()
            for head in range(own.shape[1] // HD):
                cut = slice(head * HD, (head + 1) * HD)
                here = own[rows, cut].astype(jnp.float32)
                there = far[rows, cut].astype(jnp.float32)
                out[rows, cut] = (here + share[:, head : head + 1] * (there - here)).astype(jnp.bfloat16)
            write(step).start()
            return carry

        lax.fori_loop(0, steps, one, 0)
        for step in range(steps):
            write(step).wait()


def body(groups, tensors, new_q, new_k, new_v, cache_k, cache_v, q_gain, k_gain, cache_len, home_blocks):
    row_count, feature_count = new_q.shape
    heads = feature_count // HD
    slot_rows = cache_k.shape[0]
    slots = slot_rows // CB
    chunk = 2 if heads % 2 == 0 else 1
    half, keys = row_count, slot_rows + row_count

    far_q = lax.ppermute(new_q, "group", swap_pairs(groups))
    wide_q = new_q.astype(jnp.float32)
    wide_k = new_k.astype(jnp.float32)
    squares = jnp.stack([jnp.sum(wide_q * wide_q, axis=1), jnp.sum(wide_k * wide_k, axis=1)])
    if tensors == 2:
        squares = squares + lax.ppermute(squares, "tensor", swap_pairs(tensors))
    else:
        squares = lax.psum(squares, "tensor")
    own_squares = [squares]
    far_squares = [lax.ppermute(squares, "group", swap_pairs(groups))]
    sums = len(own_squares)

    me = lax.axis_index("group").astype(jnp.int32).reshape(1)
    q_gain = q_gain.reshape(1, feature_count)
    k_gain = k_gain.reshape(1, feature_count)
    facts = jnp.concatenate([me, cache_len, home_blocks])
    smem = [pl.BlockSpec(memory_space=pltpu.SMEM)]
    vmem = pl.BlockSpec(memory_space=pltpu.VMEM)
    anywhere = pl.BlockSpec(memory_space=pl.ANY)

    stat = jax.ShapeDtypeStruct((row_count, HD), jnp.float32)
    result = jax.ShapeDtypeStruct((row_count, feature_count), jnp.bfloat16)
    new_rows = pltpu.VMEM((row_count, feature_count), jnp.bfloat16)
    slot_space = pltpu.VMEM((slot_rows, feature_count), jnp.bfloat16)
    stat_space = pltpu.VMEM((row_count, HD), jnp.float32)
    space = [
        new_rows, slot_space, slot_space, new_rows, new_rows,
        pltpu.VMEM((row_count, feature_count + HD), jnp.bfloat16),
        stat_space, stat_space, stat_space,
        pltpu.VMEM((half, keys), jnp.float32), pltpu.VMEM((half, keys), jnp.float32),
        pltpu.VMEM((half, HD), jnp.float32), pltpu.VMEM((half, HD), jnp.float32),
        pltpu.VMEM((half, keys), jnp.bfloat16), pltpu.VMEM((half, keys), jnp.bfloat16),
        pltpu.SemaphoreType.DMA((5, heads // chunk)), pltpu.SemaphoreType.DMA((heads,)), pltpu.SemaphoreType.DMA,
    ]
    pairs = row_count * heads * CB

    def cost(blocks):
        return pl.CostEstimate(
            flops=4 * pairs * HD * blocks, bytes_accessed=4 * blocks * CB * feature_count, transcendentals=pairs * blocks
        )

    def params(size):
        return pltpu.CompilerParams(vmem_limit_bytes=size)

    far_out, far_stat, own_out, own_stat = pl.pallas_call(
        functools.partial(early_kernel, slots=slots, heads=heads, chunk=chunk, sums=sums),
        out_shape=(result, stat, result, stat),
        in_specs=smem + [vmem] * (2 * sums) + [anywhere] * 6 + [vmem] * 2,
        out_specs=(anywhere,) * 4,
        scratch_shapes=space,
        compiler_params=params(VMEM),
        cost_estimate=cost(6),
        name="early_attention",
    )(facts, *own_squares, *far_squares, new_q, far_q, cache_k, cache_v, new_k, new_v, q_gain, k_gain)
    back_out, back_stat = lax.ppermute((far_out, far_stat), "group", swap_pairs(groups))

    own_out, own_stat = pl.pallas_call(
        functools.partial(late_kernel, slots=slots, heads=heads, chunk=chunk, sums=sums),
        out_shape=(result, stat),
        in_specs=smem + [vmem] * sums + [anywhere] * 5 + [vmem] * 2 + [anywhere] * 2,
        out_specs=(anywhere,) * 2,
        scratch_shapes=space,
        input_output_aliases={8 + sums: 0, 9 + sums: 1},
        compiler_params=params(VMEM),
        cost_estimate=cost(6),
        name="late_attention",
    )(facts, *own_squares, new_q, cache_k, cache_v, new_k, new_v, q_gain, k_gain, own_out, own_stat)

    step_rows = 64
    steps = row_count // step_rows
    return pl.pallas_call(
        functools.partial(join_kernel, slots=slots, step_rows=step_rows),
        out_shape=result,
        in_specs=smem + [anywhere] + [vmem] * 3,
        out_specs=anywhere,
        scratch_shapes=[
            new_rows, new_rows, pltpu.SemaphoreType.DMA((steps,)), pltpu.SemaphoreType.DMA((steps,)),
        ],
        input_output_aliases={1: 0},
        compiler_params=params(24 * 1024 * 1024),
        name="join_parts",
    )(facts, own_out, own_stat, back_out, back_stat)


def solution(mesh):
    placed = (
        P("group", "tensor"),
        P("group", "tensor"),
        P("group", "tensor"),
        P("group", "tensor"),
        P("group", "tensor"),
        P("tensor"),
        P("tensor"),
        P(),
        P(),
    )
    return jax.shard_map(
        functools.partial(body, mesh.shape["group"], mesh.shape["tensor"]),
        mesh=mesh,
        in_specs=placed,
        out_specs=P("group", "tensor"),
        check_vma=False,
    )
```

```python
import functools
import math

import jax
import jax.numpy as jnp
from jax import lax
from jax.experimental import pallas as pl
from jax.experimental.pallas import tpu as pltpu
from jax.sharding import PartitionSpec as P

HEADS = 40
HD = 128
CB = 128
EPS = 1e-06
NEGATIVE = -1e30
SCALE = math.log2(math.e) / math.sqrt(HD)
SUM_LANE = 64
VMEM = 53 * 1024 * 1024
KEYS = 256


def swap_pairs(count):
    return [(source, source ^ 1) for source in range(count)]


def row_scale(square, width, factor):
    scale = lax.rsqrt(square / width + EPS) * factor
    pieces = []
    for start in range(0, square.shape[1], HD):
        piece = jnp.broadcast_to(scale[:, start : start + HD], (HD, HD))
        pieces.append(jnp.transpose(piece))
    return jnp.concatenate(pieces, axis=0)


def counts(facts_ref, slots):
    requests = (facts_ref.shape[0] - 1) // 2
    me = facts_ref[0]
    partner = jnp.bitwise_xor(me, 1)
    own_length, far_length = facts_ref[1 + me], facts_ref[1 + partner]
    own_home = jnp.clip(facts_ref[1 + requests + me], 1, slots)
    far_home = jnp.clip(facts_ref[1 + requests + partner], 1, slots)
    own_blocks = lax.shift_right_arithmetic(own_length + (CB - 1), 7)
    far_blocks = lax.shift_right_arithmetic(far_length + (CB - 1), 7)
    own_tail = jnp.minimum(own_length - (own_home - 1) * CB, CB)
    far_tail = far_length - (far_blocks - 1) * CB
    held = jnp.clip(far_blocks - far_home, 0, slots - own_home)
    away = jnp.clip(own_blocks - own_home, 0, slots - far_home)
    return own_home, own_tail, held, far_tail, away


def early_heads(away, heads, slots, fresh):
    result = jnp.int32(0)
    for count in range(1, slots):
        share = min(heads, 2 * math.ceil((2.25 + count) * heads / (slots + fresh + 2.25) / 2 - 0.05))
        result = jnp.where(away == count, share, result)
    return result


def total_of(refs, row):
    total = refs[0][row : row + 1, :]
    for ref in refs[1:]:
        total = total + ref[row : row + 1, :]
    return total


def lanes(head):
    return pl.ds(pl.multiple_of(head * HD, HD), HD)


class Stage:
    def __init__(self, q, q_scale, q_gain, keys, values, tail, fresh, out, stat, scratch):
        self.q, self.q_scale, self.q_gain = q, q_scale, q_gain
        self.keys, self.values, self.tail, self.fresh = keys, values, tail, fresh
        self.out, self.stat = out, stat
        self.scores, self.tops, self.weights = scratch
        self.rows = q.shape[0]
        self.cached = keys.shape[0]
        self.total = self.cached + (fresh[0].shape[0] if fresh else 0)
        self.lane = lax.broadcasted_iota(jnp.int32, (self.rows, HD), 1)

    def score(self, head, slot):
        cut = lanes(head)
        raw = self.q[:, cut].astype(jnp.float32)
        queries = (raw * self.q_scale[...] * self.q_gain[:, cut]).astype(jnp.bfloat16)
        keys = self.keys[:, cut]
        if self.fresh:
            new_k, _, k_scale, k_gain = self.fresh
            raw_k = new_k[:, cut].astype(jnp.float32)
            keys = jnp.concatenate([keys, (raw_k * k_scale[...] * k_gain[:, cut]).astype(jnp.bfloat16)], axis=0)
        top = None
        for begin in range(0, self.total, KEYS):
            scores = lax.dot_general(
                queries, keys[begin : begin + KEYS], (((1,), (1,)), ((), ())), preferred_element_type=jnp.float32
            )
            for start in range(begin, min(begin + KEYS, self.total), CB):
                column = scores[:, start - begin : start - begin + CB]
                if start == self.cached - CB:
                    column = jnp.where(self.lane < self.tail, column, NEGATIVE)
                self.scores[slot][:, start : start + CB] = column
                top = column if top is None else jnp.maximum(top, column)
            yield
        self.tops[slot][...] = jnp.broadcast_to(jnp.max(top, axis=1, keepdims=True), (self.rows, HD))

    def soften(self, head, slot):
        top = self.tops[slot][...]
        for begin in range(0, self.total, KEYS):
            for start in range(begin, min(begin + KEYS, self.total), CB):
                column = self.scores[slot][:, start : start + CB]
                self.weights[slot][:, start : start + CB] = jnp.exp2(column - top).astype(jnp.bfloat16)
            yield
        pltpu.store(self.stat, top, mask=self.lane == head)

    def alternate(self, *works):
        works = list(works)
        while works:
            for work in list(works):
                if next(work, self) is self:
                    works.remove(work)

    def mix(self, head, target, lane, slot):
        cut = lanes(head)
        values = self.values[:, cut]
        if self.fresh:
            values = jnp.concatenate([values, self.fresh[1][:, cut]], axis=0)
        wide = jnp.concatenate([values, jnp.ones_like(values)], axis=1)
        mixture = jnp.dot(self.weights[slot][:, : self.total], wide, preferred_element_type=jnp.float32)
        totals = mixture[:, HD:]
        inverse = pl.reciprocal(totals, approx=True)
        inverse = inverse * (2.0 - totals * inverse)
        self.out[:, lanes(target)] = (mixture[:, :HD] * inverse).astype(jnp.bfloat16)
        pltpu.store(self.stat, totals, mask=self.lane == lane + SUM_LANE)

    def run(self, first, last, spare, ready, done, finish=None):
        ready(first, True)
        self.alternate(self.score(first, 0))

        def step(index, carry):
            head = first + 2 * index
            second = jnp.minimum(head + 1, last - 1)
            later = jnp.minimum(head + 2, last - 1)
            paired = head + 1 < last
            ready(head + 1, False)
            ready(head + 2, False)
            self.alternate(self.score(second, 1), self.soften(head, 0))
            self.mix(head, head, head, 0)
            self.alternate(self.score(later, 0), self.soften(second, 1))
            self.mix(second, jnp.where(paired, second, spare), second, 1)
            done(head).start()

            @pl.when(paired)
            def _():
                done(second).start()

            return carry

        lax.fori_loop(0, lax.shift_right_logical(last - first + 1, 1), step, 0)
        if finish is not None:
            finish()
        lax.fori_loop(first, last, lambda head, carry: (done(head).wait(), carry)[1], 0)


def loads(arrays, chunk, heads, sems):
    width = chunk * HD

    def copies(part):
        cut = pl.ds(pl.multiple_of(part * width, width), width)
        result = []
        for index, (source, target, rows) in enumerate(arrays):
            left = source.at[:, cut] if rows is None else source.at[rows, cut]
            right = target.at[:, cut] if rows is None else target.at[pl.ds(0, rows.size), cut]
            result.append(pltpu.make_async_copy(left, right, sems.at[index, part]))
        return result

    def start(first, last, between):
        def one(part, carry):
            for copy in copies(part):
                copy.start()
            return carry

        one(first // chunk, 0)
        between()
        lax.fori_loop(first // chunk + 1, (last + chunk - 1) // chunk, one, 0)

    def ready(first, last):
        def wait(head, at_start):
            if at_start:
                wanted = True
            else:
                wanted = (head < last) & (lax.rem(head, chunk) == 0)

            @pl.when(wanted)
            def _():
                for copy in copies(head // chunk):
                    copy.wait()

        return wait

    return start, ready


def early_kernel(facts_ref, *refs, slots, heads, chunk, sums):
    own_squares, far_squares, refs = refs[:sums], refs[sums : 2 * sums], refs[2 * sums :]
    (q_any, far_q_any, k_any, v_any, nk_any, nv_any, qg, kg, far_any, far_stat_any, own_any, stat_any) = refs[:12]
    q, k, v, nk, nv, out, stat, q_scale, k_scale, s0, s1, t0, t1, w0, w1, in_sems, out_sems, stat_sem = refs[12:]
    own_home, own_tail, held, far_tail, away = counts(facts_ref, slots)
    fresh_rows = nk.shape[0]
    scratch = ((s0, s1), (t0, t1), (w0, w1))

    def writer(target):
        def copy(head):
            return pltpu.make_async_copy(out.at[:, lanes(head)], target.at[:, lanes(head)], out_sems.at[head])

        return copy

    def write_stat(target):
        return pltpu.make_async_copy(stat, target, stat_sem)

    def far_scale():
        q_scale[...] = row_scale(total_of(far_squares, 0), HEADS * HD, SCALE)

    def own_scale():
        q_scale[...] = row_scale(total_of(own_squares, 0), HEADS * HD, SCALE)
        k_scale[...] = row_scale(total_of(own_squares, 1), HEADS * HD, 1.0)

    for count in range(1, slots):

        @pl.when(held == count)
        def _():
            size = count * CB
            rows = pl.ds(pl.multiple_of(jnp.minimum(own_home, slots - count) * CB, CB), size)
            start, ready = loads([(far_q_any, q, None), (k_any, k, rows), (v_any, v, rows)], chunk, heads, in_sems)
            start(0, heads, far_scale)
            Stage(
                q, q_scale, qg, k.at[pl.ds(0, size), :], v.at[pl.ds(0, size), :], far_tail, None, out, stat, scratch
            ).run(0, heads, heads, ready(0, heads), writer(far_any), write_stat(far_stat_any).start)
            write_stat(far_stat_any).wait()

    last = early_heads(away, heads, slots, fresh_rows // CB)

    @pl.when(last > 0)
    def _():
        start, ready = loads(
            [(q_any, q, None), (k_any, k, None), (v_any, v, None), (nk_any, nk, None), (nv_any, nv, None)],
            chunk, heads, in_sems,
        )
        start(0, last, own_scale)
        Stage(q, q_scale, qg, k, v, own_tail, (nk, nv, k_scale, kg), out, stat, scratch).run(
            0, last, heads, ready(0, last), writer(own_any), write_stat(stat_any).start
        )
        write_stat(stat_any).wait()


def late_kernel(facts_ref, *refs, slots, heads, chunk, sums):
    own_squares, refs = refs[:sums], refs[sums:]
    (q_any, k_any, v_any, nk_any, nv_any, qg, kg, _, _, own_any, stat_any) = refs[:11]
    q, k, v, nk, nv, out, stat, q_scale, k_scale, s0, s1, t0, t1, w0, w1, in_sems, out_sems, stat_sem = refs[11:]
    own_home, own_tail, held, far_tail, away = counts(facts_ref, slots)
    fresh_rows = nk.shape[0]
    scratch = ((s0, s1), (t0, t1), (w0, w1))
    first = early_heads(away, heads, slots, fresh_rows // CB)

    def own_scale():
        q_scale[...] = row_scale(total_of(own_squares, 0), HEADS * HD, SCALE)
        k_scale[...] = row_scale(total_of(own_squares, 1), HEADS * HD, 1.0)

    def writer(head):
        return pltpu.make_async_copy(out.at[:, lanes(head)], own_any.at[:, lanes(head)], out_sems.at[head])

    for count in range(1, slots + 1):

        @pl.when((own_home == count) & (first < heads))
        def _():
            rows = pl.ds(0, count * CB)
            start, ready = loads(
                [(q_any, q, None), (k_any, k, rows), (v_any, v, rows), (nk_any, nk, None), (nv_any, nv, None)],
                chunk, heads, in_sems,
            )
            start(first, heads, own_scale)

            @pl.when(first > 0)
            def _():
                copy = pltpu.make_async_copy(stat_any, stat, stat_sem)
                copy.start()
                copy.wait()

            Stage(
                q, q_scale, qg, k.at[rows, :], v.at[rows, :], own_tail, (nk, nv, k_scale, kg), out, stat, scratch
            ).run(first, heads, heads, ready(first, heads), writer)

            @pl.when(away > 0)
            def _():
                copy = pltpu.make_async_copy(stat, stat_any, stat_sem)
                copy.start()
                copy.wait()


def join_kernel(facts_ref, own_any, stat, far, far_stat, out_any, own, out, in_sems, out_sems, *, slots, step_rows):
    away = counts(facts_ref, slots)[4]
    steps = own.shape[0] // step_rows

    @pl.when(away > 0)
    def _():
        def piece(step):
            return pl.ds(pl.multiple_of(step * step_rows, step_rows), step_rows)

        def read(step):
            return pltpu.make_async_copy(own_any.at[piece(step), :], own.at[piece(step), :], in_sems.at[step])

        def write(step):
            return pltpu.make_async_copy(out.at[piece(step), :], out_any.at[piece(step), :], out_sems.at[step])

        for step in range(steps):
            read(step).start()

        def one(step, carry):
            rows = piece(step)
            near, away_stat = stat[rows, :], far_stat[rows, :]
            top = jnp.maximum(near, away_stat)
            own_part = pltpu.roll(near, HD - SUM_LANE, 1) * jnp.exp2(near - top)
            far_part = pltpu.roll(away_stat, HD - SUM_LANE, 1) * jnp.exp2(away_stat - top)
            share = far_part / (own_part + far_part)
            read(step).wait()
            for head in range(own.shape[1] // HD):
                cut = slice(head * HD, (head + 1) * HD)
                here = own[rows, cut].astype(jnp.float32)
                there = far[rows, cut].astype(jnp.float32)
                out[rows, cut] = (here + share[:, head : head + 1] * (there - here)).astype(jnp.bfloat16)
            write(step).start()
            return carry

        lax.fori_loop(0, steps, one, 0)
        for step in range(steps):
            write(step).wait()


def body(groups, tensors, new_q, new_k, new_v, cache_k, cache_v, q_gain, k_gain, cache_len, home_blocks):
    row_count, feature_count = new_q.shape
    heads = feature_count // HD
    slot_rows = cache_k.shape[0]
    slots = slot_rows // CB
    chunk = 2 if heads % 2 == 0 else 1
    half, keys = row_count, slot_rows + row_count

    far_q = lax.ppermute(new_q, "group", swap_pairs(groups))
    wide_q = new_q.astype(jnp.float32)
    wide_k = new_k.astype(jnp.float32)
    squares = jnp.stack([jnp.sum(wide_q * wide_q, axis=1), jnp.sum(wide_k * wide_k, axis=1)])
    if tensors == 2:
        squares = squares + lax.ppermute(squares, "tensor", swap_pairs(tensors))
    else:
        squares = lax.psum(squares, "tensor")
    own_squares = [squares]
    far_squares = [lax.ppermute(squares, "group", swap_pairs(groups))]
    sums = len(own_squares)

    me = lax.axis_index("group").astype(jnp.int32).reshape(1)
    q_gain = q_gain.reshape(1, feature_count)
    k_gain = k_gain.reshape(1, feature_count)
    facts = jnp.concatenate([me, cache_len, home_blocks])
    smem = [pl.BlockSpec(memory_space=pltpu.SMEM)]
    vmem = pl.BlockSpec(memory_space=pltpu.VMEM)
    anywhere = pl.BlockSpec(memory_space=pl.ANY)

    stat = jax.ShapeDtypeStruct((row_count, HD), jnp.float32)
    result = jax.ShapeDtypeStruct((row_count, feature_count), jnp.bfloat16)
    new_rows = pltpu.VMEM((row_count, feature_count), jnp.bfloat16)
    slot_space = pltpu.VMEM((slot_rows, feature_count), jnp.bfloat16)
    stat_space = pltpu.VMEM((row_count, HD), jnp.float32)
    space = [
        new_rows, slot_space, slot_space, new_rows, new_rows,
        pltpu.VMEM((row_count, feature_count + HD), jnp.bfloat16),
        stat_space, stat_space, stat_space,
        pltpu.VMEM((half, keys), jnp.float32), pltpu.VMEM((half, keys), jnp.float32),
        pltpu.VMEM((half, HD), jnp.float32), pltpu.VMEM((half, HD), jnp.float32),
        pltpu.VMEM((half, keys), jnp.bfloat16), pltpu.VMEM((half, keys), jnp.bfloat16),
        pltpu.SemaphoreType.DMA((5, heads // chunk)), pltpu.SemaphoreType.DMA((heads,)), pltpu.SemaphoreType.DMA,
    ]
    pairs = row_count * heads * CB

    def cost(blocks):
        return pl.CostEstimate(
            flops=4 * pairs * HD * blocks, bytes_accessed=4 * blocks * CB * feature_count, transcendentals=pairs * blocks
        )

    def params(size):
        return pltpu.CompilerParams(vmem_limit_bytes=size)

    far_out, far_stat, own_out, own_stat = pl.pallas_call(
        functools.partial(early_kernel, slots=slots, heads=heads, chunk=chunk, sums=sums),
        out_shape=(result, stat, result, stat),
        in_specs=smem + [vmem] * (2 * sums) + [anywhere] * 6 + [vmem] * 2,
        out_specs=(anywhere,) * 4,
        scratch_shapes=space,
        compiler_params=params(VMEM),
        cost_estimate=cost(6),
        name="early_attention",
    )(facts, *own_squares, *far_squares, new_q, far_q, cache_k, cache_v, new_k, new_v, q_gain, k_gain)
    back_out, back_stat = lax.ppermute((far_out, far_stat), "group", swap_pairs(groups))

    own_out, own_stat = pl.pallas_call(
        functools.partial(late_kernel, slots=slots, heads=heads, chunk=chunk, sums=sums),
        out_shape=(result, stat),
        in_specs=smem + [vmem] * sums + [anywhere] * 5 + [vmem] * 2 + [anywhere] * 2,
        out_specs=(anywhere,) * 2,
        scratch_shapes=space,
        input_output_aliases={8 + sums: 0, 9 + sums: 1},
        compiler_params=params(VMEM),
        cost_estimate=cost(6),
        name="late_attention",
    )(facts, *own_squares, new_q, cache_k, cache_v, new_k, new_v, q_gain, k_gain, own_out, own_stat)

    step_rows = 64
    steps = row_count // step_rows
    return pl.pallas_call(
        functools.partial(join_kernel, slots=slots, step_rows=step_rows),
        out_shape=result,
        in_specs=smem + [anywhere] + [vmem] * 3,
        out_specs=anywhere,
        scratch_shapes=[
            new_rows, new_rows, pltpu.SemaphoreType.DMA((steps,)), pltpu.SemaphoreType.DMA((steps,)),
        ],
        input_output_aliases={1: 0},
        compiler_params=params(24 * 1024 * 1024),
        name="join_parts",
    )(facts, own_out, own_stat, back_out, back_stat)


def solution(mesh):
    placed = (
        P("group", "tensor"),
        P("group", "tensor"),
        P("group", "tensor"),
        P("group", "tensor"),
        P("group", "tensor"),
        P("tensor"),
        P("tensor"),
        P(),
        P(),
    )
    return jax.shard_map(
        functools.partial(body, mesh.shape["group"], mesh.shape["tensor"]),
        mesh=mesh,
        in_specs=placed,
        out_specs=P("group", "tensor"),
        check_vma=False,
    )
```

```python
import functools
import math

import jax
import jax.numpy as jnp
from jax import lax
from jax.experimental import pallas as pl
from jax.experimental.pallas import tpu as pltpu
from jax.sharding import PartitionSpec as P

HEADS = 40
HD = 128
CB = 128
EPS = 1e-06
NEGATIVE = -1e30
SCALE = math.log2(math.e) / math.sqrt(HD)
SUM_LANE = 64
VMEM = 53 * 1024 * 1024
KEYS = 256


def swap_pairs(count):
    return [(source, source ^ 1) for source in range(count)]


def row_scale(square, width, factor):
    scale = lax.rsqrt(square / width + EPS) * factor
    pieces = []
    for start in range(0, square.shape[1], HD):
        piece = jnp.broadcast_to(scale[:, start : start + HD], (HD, HD))
        pieces.append(jnp.transpose(piece))
    return jnp.concatenate(pieces, axis=0)


def counts(facts_ref, slots):
    requests = (facts_ref.shape[0] - 1) // 2
    me = facts_ref[0]
    partner = jnp.bitwise_xor(me, 1)
    own_length, far_length = facts_ref[1 + me], facts_ref[1 + partner]
    own_home = jnp.clip(facts_ref[1 + requests + me], 1, slots)
    far_home = jnp.clip(facts_ref[1 + requests + partner], 1, slots)
    own_blocks = lax.shift_right_arithmetic(own_length + (CB - 1), 7)
    far_blocks = lax.shift_right_arithmetic(far_length + (CB - 1), 7)
    own_tail = jnp.minimum(own_length - (own_home - 1) * CB, CB)
    far_tail = far_length - (far_blocks - 1) * CB
    held = jnp.clip(far_blocks - far_home, 0, slots - own_home)
    away = jnp.clip(own_blocks - own_home, 0, slots - far_home)
    return own_home, own_tail, held, far_tail, away


def early_heads(away, heads, slots, fresh):
    result = jnp.int32(0)
    for count in range(1, slots):
        share = min(heads, 2 * math.ceil((2.25 + count) * heads / (slots + fresh + 2.25) / 2 - 0.05))
        result = jnp.where(away == count, share, result)
    return result


def total_of(refs, row):
    total = refs[0][row : row + 1, :]
    for ref in refs[1:]:
        total = total + ref[row : row + 1, :]
    return total


def lanes(head):
    return pl.ds(pl.multiple_of(head * HD, HD), HD)


class Stage:
    def __init__(self, q, q_scale, q_gain, keys, values, tail, fresh, out, stat, scratch):
        self.q, self.q_scale, self.q_gain = q, q_scale, q_gain
        self.keys, self.values, self.tail, self.fresh = keys, values, tail, fresh
        self.out, self.stat = out, stat
        self.scores, self.tops, self.weights = scratch
        self.rows = q.shape[0]
        self.cached = keys.shape[0]
        self.total = self.cached + (fresh[0].shape[0] if fresh else 0)
        self.lane = lax.broadcasted_iota(jnp.int32, (self.rows, HD), 1)

    def score(self, head, slot):
        cut = lanes(head)
        raw = self.q[:, cut].astype(jnp.float32)
        queries = (raw * self.q_scale[...] * self.q_gain[:, cut]).astype(jnp.bfloat16)
        keys = self.keys[:, cut]
        if self.fresh:
            new_k, _, k_scale, k_gain = self.fresh
            raw_k = new_k[:, cut].astype(jnp.float32)
            keys = jnp.concatenate([keys, (raw_k * k_scale[...] * k_gain[:, cut]).astype(jnp.bfloat16)], axis=0)
        top = None
        for begin in range(0, self.total, KEYS):
            scores = lax.dot_general(
                queries, keys[begin : begin + KEYS], (((1,), (1,)), ((), ())), preferred_element_type=jnp.float32
            )
            for start in range(begin, min(begin + KEYS, self.total), CB):
                column = scores[:, start - begin : start - begin + CB]
                if start == self.cached - CB:
                    column = jnp.where(self.lane < self.tail, column, NEGATIVE)
                self.scores[slot][:, start : start + CB] = column
                top = column if top is None else jnp.maximum(top, column)
        self.tops[slot][...] = jnp.broadcast_to(jnp.max(top, axis=1, keepdims=True), (self.rows, HD))

    def soften(self, head, slot):
        top = self.tops[slot][...]
        for start in range(0, self.total, CB):
            column = self.scores[slot][:, start : start + CB]
            self.weights[slot][:, start : start + CB] = jnp.exp2((column - top).astype(jnp.bfloat16))
        pltpu.store(self.stat, top, mask=self.lane == head)

    def mix(self, head, target, lane, slot):
        cut = lanes(head)
        values = self.values[:, cut]
        if self.fresh:
            values = jnp.concatenate([values, self.fresh[1][:, cut]], axis=0)
        wide = jnp.concatenate([values, jnp.ones_like(values)], axis=1)
        mixture = jnp.dot(self.weights[slot][:, : self.total], wide, preferred_element_type=jnp.float32)
        totals = mixture[:, HD:]
        inverse = pl.reciprocal(totals, approx=True)
        inverse = inverse * (2.0 - totals * inverse)
        self.out[:, lanes(target)] = (mixture[:, :HD] * inverse).astype(jnp.bfloat16)
        pltpu.store(self.stat, totals, mask=self.lane == lane + SUM_LANE)

    def run(self, first, last, spare, ready, done, finish=None):
        ready(first, "keys")
        self.score(first, 0)
        ready(first, "values")
        count = last - first
        paired = lax.rem(count, 2) == 0

        def step(index, carry):
            head = first + 2 * index
            second = jnp.minimum(head + 1, last - 1)
            later = jnp.minimum(head + 2, last - 1)
            begun = index > 0
            before = jnp.maximum(head - 1, first)
            ready(head + 1)
            ready(head + 2)
            self.score(second, 1)
            self.soften(head, 0)
            self.mix(before, jnp.where(begun, before, spare), jnp.where(begun, before, SUM_LANE - 1), 1)
            self.score(later, 0)
            self.soften(second, 1)
            self.mix(head, head, head, 0)
            done(head).start()

            @pl.when(begun)
            def _():
                done(before).start()

            return carry

        lax.fori_loop(0, lax.shift_right_logical(count + 1, 1), step, 0)
        self.mix(last - 1, jnp.where(paired, last - 1, spare), last - 1, 1)

        @pl.when(paired)
        def _():
            done(last - 1).start()

        if finish is not None:
            finish()
        lax.fori_loop(first, last, lambda head, carry: (done(head).wait(), carry)[1], 0)


def loads(arrays, chunk, heads, sems):
    width = chunk * HD

    def copies(part):
        cut = pl.ds(pl.multiple_of(part * width, width), width)
        result = []
        for index, (source, target, rows) in enumerate(arrays):
            left = source.at[:, cut] if rows is None else source.at[rows, cut]
            right = target.at[:, cut] if rows is None else target.at[pl.ds(0, rows.size), cut]
            result.append(pltpu.make_async_copy(left, right, sems.at[index, part]))
        return result

    def start(first, last, between):
        def one(part, carry):
            pieces = copies(part)
            for index in (0, 1, 3, 2, 4) if len(pieces) > 3 else (0, 1, 2):
                pieces[index].start()
            return carry

        one(first // chunk, 0)
        between()
        lax.fori_loop(first // chunk + 1, (last + chunk - 1) // chunk, one, 0)

    def ready(first, last):
        def wait(head, kind=None):
            pieces = copies(head // chunk)
            if kind == "keys":
                for index in (0, 1, 3)[: len(pieces) // 2 + 1 if len(pieces) > 3 else 2]:
                    pieces[index].wait()
                return
            if kind == "values":
                for index in (2, 4)[: 2 if len(pieces) > 3 else 1]:
                    pieces[index].wait()
                return

            @pl.when((head < last) & (lax.rem(head, chunk) == 0))
            def _():
                for copy in pieces:
                    copy.wait()

        return wait

    return start, ready


def early_kernel(facts_ref, *refs, slots, heads, chunk, sums):
    own_squares, far_squares, refs = refs[:sums], refs[sums : 2 * sums], refs[2 * sums :]
    (q_any, far_q_any, k_any, v_any, nk_any, nv_any, qg, kg, far_any, far_stat_any, own_any, stat_any) = refs[:12]
    q, k, v, nk, nv, out, stat, q_scale, k_scale, s0, s1, t0, t1, w0, w1, in_sems, out_sems, stat_sem = refs[12:]
    own_home, own_tail, held, far_tail, away = counts(facts_ref, slots)
    fresh_rows = nk.shape[0]
    scratch = ((s0, s1), (t0, t1), (w0, w1))

    def writer(target):
        def copy(head):
            return pltpu.make_async_copy(out.at[:, lanes(head)], target.at[:, lanes(head)], out_sems.at[head])

        return copy

    def write_stat(target):
        return pltpu.make_async_copy(stat, target, stat_sem)

    def far_scale():
        q_scale[...] = row_scale(total_of(far_squares, 0), HEADS * HD, SCALE)

    def own_scale():
        q_scale[...] = row_scale(total_of(own_squares, 0), HEADS * HD, SCALE)
        k_scale[...] = row_scale(total_of(own_squares, 1), HEADS * HD, 1.0)

    for count in range(1, slots):

        @pl.when(held == count)
        def _():
            size = count * CB
            rows = pl.ds(pl.multiple_of(jnp.minimum(own_home, slots - count) * CB, CB), size)
            start, ready = loads([(far_q_any, q, None), (k_any, k, rows), (v_any, v, rows)], chunk, heads, in_sems)
            start(0, heads, far_scale)
            Stage(
                q, q_scale, qg, k.at[pl.ds(0, size), :], v.at[pl.ds(0, size), :], far_tail, None, out, stat, scratch
            ).run(0, heads, heads, ready(0, heads), writer(far_any), write_stat(far_stat_any).start)
            write_stat(far_stat_any).wait()

    last = early_heads(away, heads, slots, fresh_rows // CB)

    @pl.when(last > 0)
    def _():
        start, ready = loads(
            [(q_any, q, None), (k_any, k, None), (v_any, v, None), (nk_any, nk, None), (nv_any, nv, None)],
            chunk, heads, in_sems,
        )
        start(0, last, own_scale)
        Stage(q, q_scale, qg, k, v, own_tail, (nk, nv, k_scale, kg), out, stat, scratch).run(
            0, last, heads, ready(0, last), writer(own_any), write_stat(stat_any).start
        )
        write_stat(stat_any).wait()


def late_kernel(facts_ref, *refs, slots, heads, chunk, sums):
    own_squares, refs = refs[:sums], refs[sums:]
    (q_any, k_any, v_any, nk_any, nv_any, qg, kg, _, _, own_any, stat_any) = refs[:11]
    q, k, v, nk, nv, out, stat, q_scale, k_scale, s0, s1, t0, t1, w0, w1, in_sems, out_sems, stat_sem = refs[11:]
    own_home, own_tail, held, far_tail, away = counts(facts_ref, slots)
    fresh_rows = nk.shape[0]
    scratch = ((s0, s1), (t0, t1), (w0, w1))
    first = early_heads(away, heads, slots, fresh_rows // CB)

    def own_scale():
        q_scale[...] = row_scale(total_of(own_squares, 0), HEADS * HD, SCALE)
        k_scale[...] = row_scale(total_of(own_squares, 1), HEADS * HD, 1.0)

    def writer(head):
        return pltpu.make_async_copy(out.at[:, lanes(head)], own_any.at[:, lanes(head)], out_sems.at[head])

    for count in range(1, slots + 1):

        @pl.when((own_home == count) & (first < heads))
        def _():
            rows = pl.ds(0, count * CB)
            start, ready = loads(
                [(q_any, q, None), (k_any, k, rows), (v_any, v, rows), (nk_any, nk, None), (nv_any, nv, None)],
                chunk, heads, in_sems,
            )
            start(first, heads, own_scale)

            @pl.when(first > 0)
            def _():
                copy = pltpu.make_async_copy(stat_any, stat, stat_sem)
                copy.start()
                copy.wait()

            Stage(
                q, q_scale, qg, k.at[rows, :], v.at[rows, :], own_tail, (nk, nv, k_scale, kg), out, stat, scratch
            ).run(first, heads, heads, ready(first, heads), writer)

            @pl.when(away > 0)
            def _():
                copy = pltpu.make_async_copy(stat, stat_any, stat_sem)
                copy.start()
                copy.wait()


def join_kernel(facts_ref, own_any, stat, far, far_stat, out_any, own, out, in_sems, out_sems, *, slots, step_rows):
    away = counts(facts_ref, slots)[4]
    steps = own.shape[0] // step_rows

    @pl.when(away > 0)
    def _():
        def piece(step):
            return pl.ds(pl.multiple_of(step * step_rows, step_rows), step_rows)

        def read(step):
            return pltpu.make_async_copy(own_any.at[piece(step), :], own.at[piece(step), :], in_sems.at[step])

        def write(step):
            return pltpu.make_async_copy(out.at[piece(step), :], out_any.at[piece(step), :], out_sems.at[step])

        for step in range(steps):
            read(step).start()

        def one(step, carry):
            rows = piece(step)
            near, away_stat = stat[rows, :], far_stat[rows, :]
            top = jnp.maximum(near, away_stat)
            own_part = pltpu.roll(near, HD - SUM_LANE, 1) * jnp.exp2(near - top)
            far_part = pltpu.roll(away_stat, HD - SUM_LANE, 1) * jnp.exp2(away_stat - top)
            share = far_part / (own_part + far_part)
            read(step).wait()
            for head in range(own.shape[1] // HD):
                cut = slice(head * HD, (head + 1) * HD)
                here = own[rows, cut].astype(jnp.float32)
                there = far[rows, cut].astype(jnp.float32)
                out[rows, cut] = (here + share[:, head : head + 1] * (there - here)).astype(jnp.bfloat16)
            write(step).start()
            return carry

        lax.fori_loop(0, steps, one, 0)
        for step in range(steps):
            write(step).wait()


def body(groups, tensors, new_q, new_k, new_v, cache_k, cache_v, q_gain, k_gain, cache_len, home_blocks):
    row_count, feature_count = new_q.shape
    heads = feature_count // HD
    slot_rows = cache_k.shape[0]
    slots = slot_rows // CB
    chunk = 2 if heads % 2 == 0 else 1
    half, keys = row_count, slot_rows + row_count

    far_q = lax.ppermute(new_q, "group", swap_pairs(groups))
    wide_q = new_q.astype(jnp.float32)
    wide_k = new_k.astype(jnp.float32)
    squares = jnp.stack([jnp.sum(wide_q * wide_q, axis=1), jnp.sum(wide_k * wide_k, axis=1)])
    if tensors == 2:
        squares = squares + lax.ppermute(squares, "tensor", swap_pairs(tensors))
    else:
        squares = lax.psum(squares, "tensor")
    own_squares = [squares]
    far_squares = [lax.ppermute(squares, "group", swap_pairs(groups))]
    sums = len(own_squares)

    me = lax.axis_index("group").astype(jnp.int32).reshape(1)
    q_gain = q_gain.reshape(1, feature_count)
    k_gain = k_gain.reshape(1, feature_count)
    facts = jnp.concatenate([me, cache_len, home_blocks])
    smem = [pl.BlockSpec(memory_space=pltpu.SMEM)]
    vmem = pl.BlockSpec(memory_space=pltpu.VMEM)
    anywhere = pl.BlockSpec(memory_space=pl.ANY)

    stat = jax.ShapeDtypeStruct((row_count, HD), jnp.float32)
    result = jax.ShapeDtypeStruct((row_count, feature_count), jnp.bfloat16)
    new_rows = pltpu.VMEM((row_count, feature_count), jnp.bfloat16)
    slot_space = pltpu.VMEM((slot_rows, feature_count), jnp.bfloat16)
    stat_space = pltpu.VMEM((row_count, HD), jnp.float32)
    space = [
        new_rows, slot_space, slot_space, new_rows, new_rows,
        pltpu.VMEM((row_count, feature_count + HD), jnp.bfloat16),
        stat_space, stat_space, stat_space,
        pltpu.VMEM((half, keys), jnp.float32), pltpu.VMEM((half, keys), jnp.float32),
        pltpu.VMEM((half, HD), jnp.float32), pltpu.VMEM((half, HD), jnp.float32),
        pltpu.VMEM((half, keys), jnp.bfloat16), pltpu.VMEM((half, keys), jnp.bfloat16),
        pltpu.SemaphoreType.DMA((5, heads // chunk)), pltpu.SemaphoreType.DMA((heads,)), pltpu.SemaphoreType.DMA,
    ]
    pairs = row_count * heads * CB

    def cost(blocks):
        return pl.CostEstimate(
            flops=4 * pairs * HD * blocks, bytes_accessed=4 * blocks * CB * feature_count, transcendentals=pairs * blocks
        )

    def params(size):
        return pltpu.CompilerParams(vmem_limit_bytes=size)

    far_out, far_stat, own_out, own_stat = pl.pallas_call(
        functools.partial(early_kernel, slots=slots, heads=heads, chunk=chunk, sums=sums),
        out_shape=(result, stat, result, stat),
        in_specs=smem + [vmem] * (2 * sums) + [anywhere] * 6 + [vmem] * 2,
        out_specs=(anywhere,) * 4,
        scratch_shapes=space,
        compiler_params=params(VMEM),
        cost_estimate=cost(6),
        name="early_attention",
    )(facts, *own_squares, *far_squares, new_q, far_q, cache_k, cache_v, new_k, new_v, q_gain, k_gain)
    back_out, back_stat = lax.ppermute((far_out, far_stat), "group", swap_pairs(groups))

    own_out, own_stat = pl.pallas_call(
        functools.partial(late_kernel, slots=slots, heads=heads, chunk=chunk, sums=sums),
        out_shape=(result, stat),
        in_specs=smem + [vmem] * sums + [anywhere] * 5 + [vmem] * 2 + [anywhere] * 2,
        out_specs=(anywhere,) * 2,
        scratch_shapes=space,
        input_output_aliases={8 + sums: 0, 9 + sums: 1},
        compiler_params=params(VMEM),
        cost_estimate=cost(6),
        name="late_attention",
    )(facts, *own_squares, new_q, cache_k, cache_v, new_k, new_v, q_gain, k_gain, own_out, own_stat)

    step_rows = 64
    steps = row_count // step_rows
    return pl.pallas_call(
        functools.partial(join_kernel, slots=slots, step_rows=step_rows),
        out_shape=result,
        in_specs=smem + [anywhere] + [vmem] * 3,
        out_specs=anywhere,
        scratch_shapes=[
            new_rows, new_rows, pltpu.SemaphoreType.DMA((steps,)), pltpu.SemaphoreType.DMA((steps,)),
        ],
        input_output_aliases={1: 0},
        compiler_params=params(24 * 1024 * 1024),
        name="join_parts",
    )(facts, own_out, own_stat, back_out, back_stat)


def solution(mesh):
    placed = (
        P("group", "tensor"),
        P("group", "tensor"),
        P("group", "tensor"),
        P("group", "tensor"),
        P("group", "tensor"),
        P("tensor"),
        P("tensor"),
        P(),
        P(),
    )
    return jax.shard_map(
        functools.partial(body, mesh.shape["group"], mesh.shape["tensor"]),
        mesh=mesh,
        in_specs=placed,
        out_specs=P("group", "tensor"),
        check_vma=False,
    )
```

```python
import functools
import math

import jax
import jax.numpy as jnp
from jax import lax
from jax.experimental import pallas as pl
from jax.experimental.pallas import tpu as pltpu
from jax.sharding import PartitionSpec as P

HEADS = 40
HD = 128
CB = 128
EPS = 1e-06
NEGATIVE = -1e30
SCALE = math.log2(math.e) / math.sqrt(HD)
SUM_LANE = 64
VMEM = 53 * 1024 * 1024
KEYS = 256


def swap_pairs(count):
    return [(source, source ^ 1) for source in range(count)]


def row_scale(square, width, factor):
    scale = lax.rsqrt(square / width + EPS) * factor
    pieces = []
    for start in range(0, square.shape[1], HD):
        piece = jnp.broadcast_to(scale[:, start : start + HD], (HD, HD))
        pieces.append(jnp.transpose(piece))
    return jnp.concatenate(pieces, axis=0)


def counts(facts_ref, slots):
    requests = (facts_ref.shape[0] - 1) // 2
    me = facts_ref[0]
    partner = jnp.bitwise_xor(me, 1)
    own_length, far_length = facts_ref[1 + me], facts_ref[1 + partner]
    own_home = jnp.clip(facts_ref[1 + requests + me], 1, slots)
    far_home = jnp.clip(facts_ref[1 + requests + partner], 1, slots)
    own_blocks = lax.shift_right_arithmetic(own_length + (CB - 1), 7)
    far_blocks = lax.shift_right_arithmetic(far_length + (CB - 1), 7)
    own_tail = jnp.minimum(own_length - (own_home - 1) * CB, CB)
    far_tail = far_length - (far_blocks - 1) * CB
    held = jnp.clip(far_blocks - far_home, 0, slots - own_home)
    away = jnp.clip(own_blocks - own_home, 0, slots - far_home)
    return own_home, own_tail, held, far_tail, away


def early_heads(away, heads, slots, fresh):
    result = jnp.int32(0)
    for count in range(1, slots):
        share = min(heads, 2 * math.ceil((2.25 + count) * heads / (slots + fresh + 2.25) / 2 - 0.05))
        result = jnp.where(away == count, share, result)
    return result


def total_of(refs, row):
    total = refs[0][row : row + 1, :]
    for ref in refs[1:]:
        total = total + ref[row : row + 1, :]
    return total


def lanes(head):
    return pl.ds(pl.multiple_of(head * HD, HD), HD)


class Stage:
    def __init__(self, q, q_scale, q_gain, keys, values, tail, fresh, out, stat, scratch):
        self.q, self.q_scale, self.q_gain = q, q_scale, q_gain
        self.keys, self.values, self.tail, self.fresh = keys, values, tail, fresh
        self.out, self.stat = out, stat
        self.scores, self.tops, self.weights, self.sums = scratch
        self.rows = q.shape[0]
        self.cached = keys.shape[0]
        self.total = self.cached + (fresh[0].shape[0] if fresh else 0)
        self.lane = lax.broadcasted_iota(jnp.int32, (self.rows, HD), 1)

    def score(self, head, slot):
        cut = lanes(head)
        raw = self.q[:, cut].astype(jnp.float32)
        queries = (raw * self.q_scale[...] * self.q_gain[:, cut]).astype(jnp.bfloat16)
        keys = self.keys[:, cut]
        if self.fresh:
            new_k, _, k_scale, k_gain = self.fresh
            raw_k = new_k[:, cut].astype(jnp.float32)
            keys = jnp.concatenate([keys, (raw_k * k_scale[...] * k_gain[:, cut]).astype(jnp.bfloat16)], axis=0)
        top = None
        for begin in range(0, self.total, KEYS):
            scores = lax.dot_general(
                queries, keys[begin : begin + KEYS], (((1,), (1,)), ((), ())), preferred_element_type=jnp.float32
            )
            for start in range(begin, min(begin + KEYS, self.total), CB):
                column = scores[:, start - begin : start - begin + CB]
                if start == self.cached - CB:
                    column = jnp.where(self.lane < self.tail, column, NEGATIVE)
                self.scores[slot][:, start : start + CB] = column
                top = column if top is None else jnp.maximum(top, column)
        self.tops[slot][...] = jnp.broadcast_to(jnp.max(top, axis=1, keepdims=True), (self.rows, HD))

    def soften(self, head, slot):
        top = self.tops[slot][...]
        total = None
        for start in range(0, self.total, CB):
            weights = jnp.exp2(self.scores[slot][:, start : start + CB] - top)
            self.weights[slot][:, start : start + CB] = weights.astype(jnp.bfloat16)
            total = weights if total is None else total + weights
        total = jnp.broadcast_to(jnp.sum(total, axis=1, keepdims=True), (self.rows, HD))
        self.sums[slot][...] = total
        pltpu.store(self.stat, top, mask=self.lane == head)
        pltpu.store(self.stat, total, mask=self.lane == head + SUM_LANE)

    def mix(self, head, target, slot):
        cut = lanes(head)
        values = self.values[:, cut]
        if self.fresh:
            values = jnp.concatenate([values, self.fresh[1][:, cut]], axis=0)
        mixture = jnp.dot(self.weights[slot][:, : self.total], values, preferred_element_type=jnp.float32)
        totals = self.sums[slot][...]
        inverse = pl.reciprocal(totals, approx=True)
        inverse = inverse * (2.0 - totals * inverse)
        self.out[:, lanes(target)] = (mixture * inverse).astype(jnp.bfloat16)

    def run(self, first, last, spare, ready, done, finish=None):
        ready(first, True)
        self.score(first, 0)
        count = last - first
        paired = lax.rem(count, 2) == 0

        def step(index, carry):
            head = first + 2 * index
            second = jnp.minimum(head + 1, last - 1)
            later = jnp.minimum(head + 2, last - 1)
            begun = index > 0
            before = jnp.maximum(head - 1, first)
            ready(head + 1, False)
            ready(head + 2, False)
            self.score(second, 1)
            self.soften(head, 0)
            self.mix(before, jnp.where(begun, before, spare), 1)
            self.score(later, 0)
            self.soften(second, 1)
            self.mix(head, head, 0)
            done(head).start()

            @pl.when(begun)
            def _():
                done(before).start()

            return carry

        lax.fori_loop(0, lax.shift_right_logical(count + 1, 1), step, 0)
        self.mix(last - 1, jnp.where(paired, last - 1, spare), 1)

        @pl.when(paired)
        def _():
            done(last - 1).start()

        if finish is not None:
            finish()
        lax.fori_loop(first, last, lambda head, carry: (done(head).wait(), carry)[1], 0)


def loads(arrays, chunk, heads, sems):
    width = chunk * HD

    def copies(part):
        cut = pl.ds(pl.multiple_of(part * width, width), width)
        result = []
        for index, (source, target, rows) in enumerate(arrays):
            left = source.at[:, cut] if rows is None else source.at[rows, cut]
            right = target.at[:, cut] if rows is None else target.at[pl.ds(0, rows.size), cut]
            result.append(pltpu.make_async_copy(left, right, sems.at[index, part]))
        return result

    def start(first, last, between):
        def one(part, carry):
            for copy in copies(part):
                copy.start()
            return carry

        one(first // chunk, 0)
        between()
        lax.fori_loop(first // chunk + 1, (last + chunk - 1) // chunk, one, 0)

    def ready(first, last):
        def wait(head, at_start):
            if at_start:
                wanted = True
            else:
                wanted = (head < last) & (lax.rem(head, chunk) == 0)

            @pl.when(wanted)
            def _():
                for copy in copies(head // chunk):
                    copy.wait()

        return wait

    return start, ready


def early_kernel(facts_ref, *refs, slots, heads, chunk, sums):
    own_squares, far_squares, refs = refs[:sums], refs[sums : 2 * sums], refs[2 * sums :]
    (q_any, far_q_any, k_any, v_any, nk_any, nv_any, qg, kg, far_any, far_stat_any, own_any, stat_any) = refs[:12]
    q, k, v, nk, nv, out, stat, q_scale, k_scale, s0, s1, t0, t1, w0, w1, u0, u1, in_sems, out_sems, stat_sem = refs[12:]
    own_home, own_tail, held, far_tail, away = counts(facts_ref, slots)
    fresh_rows = nk.shape[0]
    scratch = ((s0, s1), (t0, t1), (w0, w1), (u0, u1))

    def writer(target):
        def copy(head):
            return pltpu.make_async_copy(out.at[:, lanes(head)], target.at[:, lanes(head)], out_sems.at[head])

        return copy

    def write_stat(target):
        return pltpu.make_async_copy(stat, target, stat_sem)

    def far_scale():
        q_scale[...] = row_scale(total_of(far_squares, 0), HEADS * HD, SCALE)

    def own_scale():
        q_scale[...] = row_scale(total_of(own_squares, 0), HEADS * HD, SCALE)
        k_scale[...] = row_scale(total_of(own_squares, 1), HEADS * HD, 1.0)

    for count in range(1, slots):

        @pl.when(held == count)
        def _():
            size = count * CB
            rows = pl.ds(pl.multiple_of(jnp.minimum(own_home, slots - count) * CB, CB), size)
            start, ready = loads([(far_q_any, q, None), (k_any, k, rows), (v_any, v, rows)], chunk, heads, in_sems)
            start(0, heads, far_scale)
            Stage(
                q, q_scale, qg, k.at[pl.ds(0, size), :], v.at[pl.ds(0, size), :], far_tail, None, out, stat, scratch
            ).run(0, heads, heads, ready(0, heads), writer(far_any), write_stat(far_stat_any).start)
            write_stat(far_stat_any).wait()

    last = early_heads(away, heads, slots, fresh_rows // CB)

    @pl.when(last > 0)
    def _():
        start, ready = loads(
            [(q_any, q, None), (k_any, k, None), (v_any, v, None), (nk_any, nk, None), (nv_any, nv, None)],
            chunk, heads, in_sems,
        )
        start(0, last, own_scale)
        Stage(q, q_scale, qg, k, v, own_tail, (nk, nv, k_scale, kg), out, stat, scratch).run(
            0, last, heads, ready(0, last), writer(own_any), write_stat(stat_any).start
        )
        write_stat(stat_any).wait()


def late_kernel(facts_ref, *refs, slots, heads, chunk, sums):
    own_squares, refs = refs[:sums], refs[sums:]
    (q_any, k_any, v_any, nk_any, nv_any, qg, kg, _, _, own_any, stat_any) = refs[:11]
    q, k, v, nk, nv, out, stat, q_scale, k_scale, s0, s1, t0, t1, w0, w1, u0, u1, in_sems, out_sems, stat_sem = refs[11:]
    own_home, own_tail, held, far_tail, away = counts(facts_ref, slots)
    fresh_rows = nk.shape[0]
    scratch = ((s0, s1), (t0, t1), (w0, w1), (u0, u1))
    first = early_heads(away, heads, slots, fresh_rows // CB)

    def own_scale():
        q_scale[...] = row_scale(total_of(own_squares, 0), HEADS * HD, SCALE)
        k_scale[...] = row_scale(total_of(own_squares, 1), HEADS * HD, 1.0)

    def writer(head):
        return pltpu.make_async_copy(out.at[:, lanes(head)], own_any.at[:, lanes(head)], out_sems.at[head])

    for count in range(1, slots + 1):

        @pl.when((own_home == count) & (first < heads))
        def _():
            rows = pl.ds(0, count * CB)
            start, ready = loads(
                [(q_any, q, None), (k_any, k, rows), (v_any, v, rows), (nk_any, nk, None), (nv_any, nv, None)],
                chunk, heads, in_sems,
            )
            start(first, heads, own_scale)

            @pl.when(first > 0)
            def _():
                copy = pltpu.make_async_copy(stat_any, stat, stat_sem)
                copy.start()
                copy.wait()

            Stage(
                q, q_scale, qg, k.at[rows, :], v.at[rows, :], own_tail, (nk, nv, k_scale, kg), out, stat, scratch
            ).run(first, heads, heads, ready(first, heads), writer)

            @pl.when(away > 0)
            def _():
                copy = pltpu.make_async_copy(stat, stat_any, stat_sem)
                copy.start()
                copy.wait()


def join_kernel(facts_ref, own_any, stat, far, far_stat, out_any, own, out, in_sems, out_sems, *, slots, step_rows):
    away = counts(facts_ref, slots)[4]
    steps = own.shape[0] // step_rows

    @pl.when(away > 0)
    def _():
        def piece(step):
            return pl.ds(pl.multiple_of(step * step_rows, step_rows), step_rows)

        def read(step):
            return pltpu.make_async_copy(own_any.at[piece(step), :], own.at[piece(step), :], in_sems.at[step])

        def write(step):
            return pltpu.make_async_copy(out.at[piece(step), :], out_any.at[piece(step), :], out_sems.at[step])

        for step in range(steps):
            read(step).start()

        def one(step, carry):
            rows = piece(step)
            near, away_stat = stat[rows, :], far_stat[rows, :]
            top = jnp.maximum(near, away_stat)
            own_part = pltpu.roll(near, HD - SUM_LANE, 1) * jnp.exp2(near - top)
            far_part = pltpu.roll(away_stat, HD - SUM_LANE, 1) * jnp.exp2(away_stat - top)
            share = far_part / (own_part + far_part)
            read(step).wait()
            for head in range(own.shape[1] // HD):
                cut = slice(head * HD, (head + 1) * HD)
                here = own[rows, cut].astype(jnp.float32)
                there = far[rows, cut].astype(jnp.float32)
                out[rows, cut] = (here + share[:, head : head + 1] * (there - here)).astype(jnp.bfloat16)
            write(step).start()
            return carry

        lax.fori_loop(0, steps, one, 0)
        for step in range(steps):
            write(step).wait()


def body(groups, tensors, new_q, new_k, new_v, cache_k, cache_v, q_gain, k_gain, cache_len, home_blocks):
    row_count, feature_count = new_q.shape
    heads = feature_count // HD
    slot_rows = cache_k.shape[0]
    slots = slot_rows // CB
    chunk = 2 if heads % 2 == 0 else 1
    half, keys = row_count, slot_rows + row_count

    far_q = lax.ppermute(new_q, "group", swap_pairs(groups))
    wide_q = new_q.astype(jnp.float32)
    wide_k = new_k.astype(jnp.float32)
    squares = jnp.stack([jnp.sum(wide_q * wide_q, axis=1), jnp.sum(wide_k * wide_k, axis=1)])
    if tensors == 2:
        squares = squares + lax.ppermute(squares, "tensor", swap_pairs(tensors))
    else:
        squares = lax.psum(squares, "tensor")
    own_squares = [squares]
    far_squares = [lax.ppermute(squares, "group", swap_pairs(groups))]
    sums = len(own_squares)

    me = lax.axis_index("group").astype(jnp.int32).reshape(1)
    q_gain = q_gain.reshape(1, feature_count)
    k_gain = k_gain.reshape(1, feature_count)
    facts = jnp.concatenate([me, cache_len, home_blocks])
    smem = [pl.BlockSpec(memory_space=pltpu.SMEM)]
    vmem = pl.BlockSpec(memory_space=pltpu.VMEM)
    anywhere = pl.BlockSpec(memory_space=pl.ANY)

    stat = jax.ShapeDtypeStruct((row_count, HD), jnp.float32)
    result = jax.ShapeDtypeStruct((row_count, feature_count), jnp.bfloat16)
    new_rows = pltpu.VMEM((row_count, feature_count), jnp.bfloat16)
    slot_space = pltpu.VMEM((slot_rows, feature_count), jnp.bfloat16)
    stat_space = pltpu.VMEM((row_count, HD), jnp.float32)
    space = [
        new_rows, slot_space, slot_space, new_rows, new_rows,
        pltpu.VMEM((row_count, feature_count + HD), jnp.bfloat16),
        stat_space, stat_space, stat_space,
        pltpu.VMEM((half, keys), jnp.float32), pltpu.VMEM((half, keys), jnp.float32),
        pltpu.VMEM((half, HD), jnp.float32), pltpu.VMEM((half, HD), jnp.float32),
        pltpu.VMEM((half, keys), jnp.bfloat16), pltpu.VMEM((half, keys), jnp.bfloat16),
        stat_space, stat_space,
        pltpu.SemaphoreType.DMA((5, heads // chunk)), pltpu.SemaphoreType.DMA((heads,)), pltpu.SemaphoreType.DMA,
    ]
    pairs = row_count * heads * CB

    def cost(blocks):
        return pl.CostEstimate(
            flops=4 * pairs * HD * blocks, bytes_accessed=4 * blocks * CB * feature_count, transcendentals=pairs * blocks
        )

    def params(size):
        return pltpu.CompilerParams(vmem_limit_bytes=size)

    far_out, far_stat, own_out, own_stat = pl.pallas_call(
        functools.partial(early_kernel, slots=slots, heads=heads, chunk=chunk, sums=sums),
        out_shape=(result, stat, result, stat),
        in_specs=smem + [vmem] * (2 * sums) + [anywhere] * 6 + [vmem] * 2,
        out_specs=(anywhere,) * 4,
        scratch_shapes=space,
        compiler_params=params(VMEM),
        cost_estimate=cost(6),
        name="early_attention",
    )(facts, *own_squares, *far_squares, new_q, far_q, cache_k, cache_v, new_k, new_v, q_gain, k_gain)
    back_out, back_stat = lax.ppermute((far_out, far_stat), "group", swap_pairs(groups))

    own_out, own_stat = pl.pallas_call(
        functools.partial(late_kernel, slots=slots, heads=heads, chunk=chunk, sums=sums),
        out_shape=(result, stat),
        in_specs=smem + [vmem] * sums + [anywhere] * 5 + [vmem] * 2 + [anywhere] * 2,
        out_specs=(anywhere,) * 2,
        scratch_shapes=space,
        input_output_aliases={8 + sums: 0, 9 + sums: 1},
        compiler_params=params(VMEM),
        cost_estimate=cost(6),
        name="late_attention",
    )(facts, *own_squares, new_q, cache_k, cache_v, new_k, new_v, q_gain, k_gain, own_out, own_stat)

    step_rows = 64
    steps = row_count // step_rows
    return pl.pallas_call(
        functools.partial(join_kernel, slots=slots, step_rows=step_rows),
        out_shape=result,
        in_specs=smem + [anywhere] + [vmem] * 3,
        out_specs=anywhere,
        scratch_shapes=[
            new_rows, new_rows, pltpu.SemaphoreType.DMA((steps,)), pltpu.SemaphoreType.DMA((steps,)),
        ],
        input_output_aliases={1: 0},
        compiler_params=params(24 * 1024 * 1024),
        name="join_parts",
    )(facts, own_out, own_stat, back_out, back_stat)


def solution(mesh):
    placed = (
        P("group", "tensor"),
        P("group", "tensor"),
        P("group", "tensor"),
        P("group", "tensor"),
        P("group", "tensor"),
        P("tensor"),
        P("tensor"),
        P(),
        P(),
    )
    return jax.shard_map(
        functools.partial(body, mesh.shape["group"], mesh.shape["tensor"]),
        mesh=mesh,
        in_specs=placed,
        out_specs=P("group", "tensor"),
        check_vma=False,
    )
```

```python
import functools
import math

import jax
import jax.numpy as jnp
from jax import lax
from jax.experimental import pallas as pl
from jax.experimental.pallas import tpu as pltpu
from jax.sharding import PartitionSpec as P

HEADS = 40
HD = 128
CB = 128
EPS = 1e-06
NEGATIVE = -1e30
SCALE = math.log2(math.e) / math.sqrt(HD)
SUM_LANE = 64
VMEM = 53 * 1024 * 1024
KEYS = 512
PIECE = 64


def swap_pairs(count):
    return [(source, source ^ 1) for source in range(count)]


def row_scale(square, width, factor):
    scale = lax.rsqrt(square / width + EPS) * factor
    pieces = []
    for start in range(0, square.shape[1], HD):
        piece = jnp.broadcast_to(scale[:, start : start + HD], (HD, HD))
        pieces.append(jnp.transpose(piece))
    return jnp.concatenate(pieces, axis=0)


def counts(facts_ref, slots):
    requests = (facts_ref.shape[0] - 1) // 2
    me = facts_ref[0]
    partner = jnp.bitwise_xor(me, 1)
    own_length, far_length = facts_ref[1 + me], facts_ref[1 + partner]
    own_home = jnp.clip(facts_ref[1 + requests + me], 1, slots)
    far_home = jnp.clip(facts_ref[1 + requests + partner], 1, slots)
    own_blocks = lax.shift_right_arithmetic(own_length + (CB - 1), 7)
    far_blocks = lax.shift_right_arithmetic(far_length + (CB - 1), 7)
    own_tail = jnp.minimum(own_length - (own_home - 1) * CB, CB)
    far_tail = far_length - (far_blocks - 1) * CB
    held = jnp.clip(far_blocks - far_home, 0, slots - own_home)
    away = jnp.clip(own_blocks - own_home, 0, slots - far_home)
    return own_home, own_tail, held, far_tail, away


def early_heads(away, heads, slots, fresh):
    result = jnp.int32(0)
    for count in range(1, slots):
        share = min(heads, 2 * math.ceil((2.25 + count) * heads / (slots + fresh + 2.25) / 2 - 0.05))
        result = jnp.where(away == count, share, result)
    return result


def total_of(refs, row):
    total = refs[0][row : row + 1, :]
    for ref in refs[1:]:
        total = total + ref[row : row + 1, :]
    return total


def lanes(head):
    return pl.ds(pl.multiple_of(head * HD, HD), HD)


class Stage:
    def __init__(self, q, q_scale, q_gain, keys, values, tail, fresh, out, stat, scratch):
        self.q, self.q_scale, self.q_gain = q, q_scale, q_gain
        self.keys, self.values, self.tail, self.fresh = keys, values, tail, fresh
        self.out, self.stat = out, stat
        self.scores, self.tops, self.weights = scratch
        self.rows = q.shape[0]
        self.cached = keys.shape[0]
        self.total = self.cached + (fresh[0].shape[0] if fresh else 0)
        self.lane = lax.broadcasted_iota(jnp.int32, (self.rows, HD), 1)

    def score(self, head, slot):
        cut = lanes(head)
        raw = self.q[:, cut].astype(jnp.float32)
        queries = (raw * self.q_scale[...] * self.q_gain[:, cut]).astype(jnp.bfloat16)
        keys = self.keys[:, cut]
        if self.fresh:
            new_k, _, k_scale, k_gain = self.fresh
            raw_k = new_k[:, cut].astype(jnp.float32)
            keys = jnp.concatenate([keys, (raw_k * k_scale[...] * k_gain[:, cut]).astype(jnp.bfloat16)], axis=0)
        tops = [None] * (self.rows // PIECE)
        lane = self.lane[:PIECE]
        for begin in range(0, self.total, KEYS):
            scores = lax.dot_general(
                queries, keys[begin : begin + KEYS], (((1,), (1,)), ((), ())), preferred_element_type=jnp.float32
            )
            for index in range(len(tops)):
                piece = slice(index * PIECE, (index + 1) * PIECE)
                top = tops[index]
                for start in range(begin, min(begin + KEYS, self.total), CB):
                    column = scores[piece, start - begin : start - begin + CB]
                    if start == self.cached - CB:
                        column = jnp.where(lane < self.tail, column, NEGATIVE)
                    self.scores[slot][piece, start : start + CB] = column
                    top = column if top is None else jnp.maximum(top, column)
                tops[index] = top
        for index, top in enumerate(tops):
            piece = slice(index * PIECE, (index + 1) * PIECE)
            self.tops[slot][piece, :] = jnp.broadcast_to(jnp.max(top, axis=1, keepdims=True), (PIECE, HD))

    def soften(self, head, slot):
        top = self.tops[slot][...]
        for start in range(0, self.total, CB):
            column = self.scores[slot][:, start : start + CB]
            self.weights[slot][:, start : start + CB] = jnp.exp2(column - top).astype(jnp.bfloat16)
        pltpu.store(self.stat, top, mask=self.lane == head)

    def mix(self, head, target, lane, slot):
        cut = lanes(head)
        values = self.values[:, cut]
        if self.fresh:
            values = jnp.concatenate([values, self.fresh[1][:, cut]], axis=0)
        wide = jnp.concatenate([values, jnp.ones_like(values)], axis=1)
        mixture = jnp.dot(self.weights[slot][:, : self.total], wide, preferred_element_type=jnp.float32)
        totals = mixture[:, HD:]
        inverse = pl.reciprocal(totals, approx=True)
        inverse = inverse * (2.0 - totals * inverse)
        self.out[:, lanes(target)] = (mixture[:, :HD] * inverse).astype(jnp.bfloat16)
        pltpu.store(self.stat, totals, mask=self.lane == lane + SUM_LANE)

    def run(self, first, last, spare, ready, done, finish=None):
        ready(first, True)
        self.score(first, 0)
        count = last - first
        paired = lax.rem(count, 2) == 0

        def step(index, carry):
            head = first + 2 * index
            second = jnp.minimum(head + 1, last - 1)
            later = jnp.minimum(head + 2, last - 1)
            begun = index > 0
            before = jnp.maximum(head - 1, first)
            ready(head + 1, False)
            ready(head + 2, False)
            self.score(second, 1)
            self.soften(head, 0)
            self.mix(before, jnp.where(begun, before, spare), jnp.where(begun, before, SUM_LANE - 1), 1)
            self.score(later, 0)
            self.soften(second, 1)
            self.mix(head, head, head, 0)
            done(head).start()

            @pl.when(begun)
            def _():
                done(before).start()

            return carry

        lax.fori_loop(0, lax.shift_right_logical(count + 1, 1), step, 0)
        self.mix(last - 1, jnp.where(paired, last - 1, spare), last - 1, 1)

        @pl.when(paired)
        def _():
            done(last - 1).start()

        if finish is not None:
            finish()
        lax.fori_loop(first, last, lambda head, carry: (done(head).wait(), carry)[1], 0)


def loads(arrays, chunk, heads, sems):
    width = chunk * HD

    def copies(part):
        cut = pl.ds(pl.multiple_of(part * width, width), width)
        result = []
        for index, (source, target, rows) in enumerate(arrays):
            left = source.at[:, cut] if rows is None else source.at[rows, cut]
            right = target.at[:, cut] if rows is None else target.at[pl.ds(0, rows.size), cut]
            result.append(pltpu.make_async_copy(left, right, sems.at[index, part]))
        return result

    def start(first, last, between):
        def one(part, carry):
            for copy in copies(part):
                copy.start()
            return carry

        one(first // chunk, 0)
        between()
        lax.fori_loop(first // chunk + 1, (last + chunk - 1) // chunk, one, 0)

    def ready(first, last):
        def wait(head, at_start):
            if at_start:
                wanted = True
            else:
                wanted = (head < last) & (lax.rem(head, chunk) == 0)

            @pl.when(wanted)
            def _():
                for copy in copies(head // chunk):
                    copy.wait()

        return wait

    return start, ready


def early_kernel(facts_ref, *refs, slots, heads, chunk, sums):
    own_squares, far_squares, refs = refs[:sums], refs[sums : 2 * sums], refs[2 * sums :]
    (q_any, far_q_any, k_any, v_any, nk_any, nv_any, qg, kg, far_any, far_stat_any, own_any, stat_any) = refs[:12]
    q, k, v, nk, nv, out, stat, q_scale, k_scale, s0, s1, t0, t1, w0, w1, in_sems, out_sems, stat_sem = refs[12:]
    own_home, own_tail, held, far_tail, away = counts(facts_ref, slots)
    fresh_rows = nk.shape[0]
    scratch = ((s0, s1), (t0, t1), (w0, w1))

    def writer(target):
        def copy(head):
            return pltpu.make_async_copy(out.at[:, lanes(head)], target.at[:, lanes(head)], out_sems.at[head])

        return copy

    def write_stat(target):
        return pltpu.make_async_copy(stat, target, stat_sem)

    def far_scale():
        q_scale[...] = row_scale(total_of(far_squares, 0), HEADS * HD, SCALE)

    def own_scale():
        q_scale[...] = row_scale(total_of(own_squares, 0), HEADS * HD, SCALE)
        k_scale[...] = row_scale(total_of(own_squares, 1), HEADS * HD, 1.0)

    for count in range(1, slots):

        @pl.when(held == count)
        def _():
            size = count * CB
            rows = pl.ds(pl.multiple_of(jnp.minimum(own_home, slots - count) * CB, CB), size)
            start, ready = loads([(far_q_any, q, None), (k_any, k, rows), (v_any, v, rows)], chunk, heads, in_sems)
            start(0, heads, far_scale)
            Stage(
                q, q_scale, qg, k.at[pl.ds(0, size), :], v.at[pl.ds(0, size), :], far_tail, None, out, stat, scratch
            ).run(0, heads, heads, ready(0, heads), writer(far_any), write_stat(far_stat_any).start)
            write_stat(far_stat_any).wait()

    last = early_heads(away, heads, slots, fresh_rows // CB)

    @pl.when(last > 0)
    def _():
        start, ready = loads(
            [(q_any, q, None), (k_any, k, None), (v_any, v, None), (nk_any, nk, None), (nv_any, nv, None)],
            chunk, heads, in_sems,
        )
        start(0, last, own_scale)
        Stage(q, q_scale, qg, k, v, own_tail, (nk, nv, k_scale, kg), out, stat, scratch).run(
            0, last, heads, ready(0, last), writer(own_any), write_stat(stat_any).start
        )
        write_stat(stat_any).wait()


def late_kernel(facts_ref, *refs, slots, heads, chunk, sums):
    own_squares, refs = refs[:sums], refs[sums:]
    (q_any, k_any, v_any, nk_any, nv_any, qg, kg, _, _, own_any, stat_any) = refs[:11]
    q, k, v, nk, nv, out, stat, q_scale, k_scale, s0, s1, t0, t1, w0, w1, in_sems, out_sems, stat_sem = refs[11:]
    own_home, own_tail, held, far_tail, away = counts(facts_ref, slots)
    fresh_rows = nk.shape[0]
    scratch = ((s0, s1), (t0, t1), (w0, w1))
    first = early_heads(away, heads, slots, fresh_rows // CB)

    def own_scale():
        q_scale[...] = row_scale(total_of(own_squares, 0), HEADS * HD, SCALE)
        k_scale[...] = row_scale(total_of(own_squares, 1), HEADS * HD, 1.0)

    def writer(head):
        return pltpu.make_async_copy(out.at[:, lanes(head)], own_any.at[:, lanes(head)], out_sems.at[head])

    for count in range(1, slots + 1):

        @pl.when((own_home == count) & (first < heads))
        def _():
            rows = pl.ds(0, count * CB)
            start, ready = loads(
                [(q_any, q, None), (k_any, k, rows), (v_any, v, rows), (nk_any, nk, None), (nv_any, nv, None)],
                chunk, heads, in_sems,
            )
            start(first, heads, own_scale)

            @pl.when(first > 0)
            def _():
                copy = pltpu.make_async_copy(stat_any, stat, stat_sem)
                copy.start()
                copy.wait()

            Stage(
                q, q_scale, qg, k.at[rows, :], v.at[rows, :], own_tail, (nk, nv, k_scale, kg), out, stat, scratch
            ).run(first, heads, heads, ready(first, heads), writer)

            @pl.when(away > 0)
            def _():
                copy = pltpu.make_async_copy(stat, stat_any, stat_sem)
                copy.start()
                copy.wait()


def join_kernel(facts_ref, own_any, stat, far, far_stat, out_any, own, out, in_sems, out_sems, *, slots, step_rows):
    away = counts(facts_ref, slots)[4]
    steps = own.shape[0] // step_rows

    @pl.when(away > 0)
    def _():
        def piece(step):
            return pl.ds(pl.multiple_of(step * step_rows, step_rows), step_rows)

        def read(step):
            return pltpu.make_async_copy(own_any.at[piece(step), :], own.at[piece(step), :], in_sems.at[step])

        def write(step):
            return pltpu.make_async_copy(out.at[piece(step), :], out_any.at[piece(step), :], out_sems.at[step])

        for step in range(steps):
            read(step).start()

        def one(step, carry):
            rows = piece(step)
            near, away_stat = stat[rows, :], far_stat[rows, :]
            top = jnp.maximum(near, away_stat)
            own_part = pltpu.roll(near, HD - SUM_LANE, 1) * jnp.exp2(near - top)
            far_part = pltpu.roll(away_stat, HD - SUM_LANE, 1) * jnp.exp2(away_stat - top)
            share = far_part / (own_part + far_part)
            read(step).wait()
            for head in range(own.shape[1] // HD):
                cut = slice(head * HD, (head + 1) * HD)
                here = own[rows, cut].astype(jnp.float32)
                there = far[rows, cut].astype(jnp.float32)
                out[rows, cut] = (here + share[:, head : head + 1] * (there - here)).astype(jnp.bfloat16)
            write(step).start()
            return carry

        lax.fori_loop(0, steps, one, 0)
        for step in range(steps):
            write(step).wait()


def body(groups, tensors, new_q, new_k, new_v, cache_k, cache_v, q_gain, k_gain, cache_len, home_blocks):
    row_count, feature_count = new_q.shape
    heads = feature_count // HD
    slot_rows = cache_k.shape[0]
    slots = slot_rows // CB
    chunk = 2 if heads % 2 == 0 else 1
    half, keys = row_count, slot_rows + row_count

    far_q = lax.ppermute(new_q, "group", swap_pairs(groups))
    wide_q = new_q.astype(jnp.float32)
    wide_k = new_k.astype(jnp.float32)
    squares = jnp.stack([jnp.sum(wide_q * wide_q, axis=1), jnp.sum(wide_k * wide_k, axis=1)])
    if tensors == 2:
        squares = squares + lax.ppermute(squares, "tensor", swap_pairs(tensors))
    else:
        squares = lax.psum(squares, "tensor")
    own_squares = [squares]
    far_squares = [lax.ppermute(squares, "group", swap_pairs(groups))]
    sums = len(own_squares)

    me = lax.axis_index("group").astype(jnp.int32).reshape(1)
    q_gain = q_gain.reshape(1, feature_count)
    k_gain = k_gain.reshape(1, feature_count)
    facts = jnp.concatenate([me, cache_len, home_blocks])
    smem = [pl.BlockSpec(memory_space=pltpu.SMEM)]
    vmem = pl.BlockSpec(memory_space=pltpu.VMEM)
    anywhere = pl.BlockSpec(memory_space=pl.ANY)

    stat = jax.ShapeDtypeStruct((row_count, HD), jnp.float32)
    result = jax.ShapeDtypeStruct((row_count, feature_count), jnp.bfloat16)
    new_rows = pltpu.VMEM((row_count, feature_count), jnp.bfloat16)
    slot_space = pltpu.VMEM((slot_rows, feature_count), jnp.bfloat16)
    stat_space = pltpu.VMEM((row_count, HD), jnp.float32)
    space = [
        new_rows, slot_space, slot_space, new_rows, new_rows,
        pltpu.VMEM((row_count, feature_count + HD), jnp.bfloat16),
        stat_space, stat_space, stat_space,
        pltpu.VMEM((half, keys), jnp.float32), pltpu.VMEM((half, keys), jnp.float32),
        pltpu.VMEM((half, HD), jnp.float32), pltpu.VMEM((half, HD), jnp.float32),
        pltpu.VMEM((half, keys), jnp.bfloat16), pltpu.VMEM((half, keys), jnp.bfloat16),
        pltpu.SemaphoreType.DMA((5, heads // chunk)), pltpu.SemaphoreType.DMA((heads,)), pltpu.SemaphoreType.DMA,
    ]
    pairs = row_count * heads * CB

    def cost(blocks):
        return pl.CostEstimate(
            flops=4 * pairs * HD * blocks, bytes_accessed=4 * blocks * CB * feature_count, transcendentals=pairs * blocks
        )

    def params(size):
        return pltpu.CompilerParams(vmem_limit_bytes=size)

    far_out, far_stat, own_out, own_stat = pl.pallas_call(
        functools.partial(early_kernel, slots=slots, heads=heads, chunk=chunk, sums=sums),
        out_shape=(result, stat, result, stat),
        in_specs=smem + [vmem] * (2 * sums) + [anywhere] * 6 + [vmem] * 2,
        out_specs=(anywhere,) * 4,
        scratch_shapes=space,
        compiler_params=params(VMEM),
        cost_estimate=cost(6),
        name="early_attention",
    )(facts, *own_squares, *far_squares, new_q, far_q, cache_k, cache_v, new_k, new_v, q_gain, k_gain)
    back_out, back_stat = lax.ppermute((far_out, far_stat), "group", swap_pairs(groups))

    own_out, own_stat = pl.pallas_call(
        functools.partial(late_kernel, slots=slots, heads=heads, chunk=chunk, sums=sums),
        out_shape=(result, stat),
        in_specs=smem + [vmem] * sums + [anywhere] * 5 + [vmem] * 2 + [anywhere] * 2,
        out_specs=(anywhere,) * 2,
        scratch_shapes=space,
        input_output_aliases={8 + sums: 0, 9 + sums: 1},
        compiler_params=params(VMEM),
        cost_estimate=cost(6),
        name="late_attention",
    )(facts, *own_squares, new_q, cache_k, cache_v, new_k, new_v, q_gain, k_gain, own_out, own_stat)

    step_rows = 64
    steps = row_count // step_rows
    return pl.pallas_call(
        functools.partial(join_kernel, slots=slots, step_rows=step_rows),
        out_shape=result,
        in_specs=smem + [anywhere] + [vmem] * 3,
        out_specs=anywhere,
        scratch_shapes=[
            new_rows, new_rows, pltpu.SemaphoreType.DMA((steps,)), pltpu.SemaphoreType.DMA((steps,)),
        ],
        input_output_aliases={1: 0},
        compiler_params=params(24 * 1024 * 1024),
        name="join_parts",
    )(facts, own_out, own_stat, back_out, back_stat)


def solution(mesh):
    placed = (
        P("group", "tensor"),
        P("group", "tensor"),
        P("group", "tensor"),
        P("group", "tensor"),
        P("group", "tensor"),
        P("tensor"),
        P("tensor"),
        P(),
        P(),
    )
    return jax.shard_map(
        functools.partial(body, mesh.shape["group"], mesh.shape["tensor"]),
        mesh=mesh,
        in_specs=placed,
        out_specs=P("group", "tensor"),
        check_vma=False,
    )
```

```python
import functools
import math

import jax
import jax.numpy as jnp
from jax import lax
from jax.experimental import pallas as pl
from jax.experimental.pallas import tpu as pltpu
from jax.sharding import PartitionSpec as P

HEADS = 40
HD = 128
CB = 128
EPS = 1e-06
NEGATIVE = -1e30
SCALE = math.log2(math.e) / math.sqrt(HD)
SUM_LANE = 64
VMEM = 53 * 1024 * 1024
KEYS = 512
PIECE = 64


def swap_pairs(count):
    return [(source, source ^ 1) for source in range(count)]


def row_scale(square, width, factor):
    scale = lax.rsqrt(square / width + EPS) * factor
    pieces = []
    for start in range(0, square.shape[1], HD):
        piece = jnp.broadcast_to(scale[:, start : start + HD], (HD, HD))
        pieces.append(jnp.transpose(piece))
    return jnp.concatenate(pieces, axis=0)


def counts(facts_ref, slots):
    requests = (facts_ref.shape[0] - 1) // 2
    me = facts_ref[0]
    partner = jnp.bitwise_xor(me, 1)
    own_length, far_length = facts_ref[1 + me], facts_ref[1 + partner]
    own_home = jnp.clip(facts_ref[1 + requests + me], 1, slots)
    far_home = jnp.clip(facts_ref[1 + requests + partner], 1, slots)
    own_blocks = lax.shift_right_arithmetic(own_length + (CB - 1), 7)
    far_blocks = lax.shift_right_arithmetic(far_length + (CB - 1), 7)
    own_tail = jnp.minimum(own_length - (own_home - 1) * CB, CB)
    far_tail = far_length - (far_blocks - 1) * CB
    held = jnp.clip(far_blocks - far_home, 0, slots - own_home)
    away = jnp.clip(own_blocks - own_home, 0, slots - far_home)
    return own_home, own_tail, held, far_tail, away


def early_heads(away, heads, slots, fresh):
    result = jnp.int32(0)
    for count in range(1, slots):
        share = min(heads, 2 * math.ceil((2.25 + count) * heads / (slots + fresh + 2.25) / 2 - 0.05))
        result = jnp.where(away == count, share, result)
    return result


def total_of(refs, row):
    total = refs[0][row : row + 1, :]
    for ref in refs[1:]:
        total = total + ref[row : row + 1, :]
    return total


def lanes(head):
    return pl.ds(pl.multiple_of(head * HD, HD), HD)


class Stage:
    def __init__(self, q, q_scale, q_gain, keys, values, tail, fresh, out, stat, scratch):
        self.q, self.q_scale, self.q_gain = q, q_scale, q_gain
        self.keys, self.values, self.tail, self.fresh = keys, values, tail, fresh
        self.out, self.stat = out, stat
        self.scores, self.tops, self.weights = scratch
        self.rows = q.shape[0]
        self.cached = keys.shape[0]
        self.total = self.cached + (fresh[0].shape[0] if fresh else 0)
        self.lane = lax.broadcasted_iota(jnp.int32, (PIECE, HD), 1)

    def note(self, values, lane):
        here = self.lane == lane
        for start in range(0, self.rows, PIECE):
            pltpu.store(self.stat.at[pl.ds(start, PIECE), :], values[start : start + PIECE], mask=here)

    def score(self, head, slot):
        cut = lanes(head)
        raw = self.q[:, cut].astype(jnp.float32)
        queries = (raw * self.q_scale[...] * self.q_gain[:, cut]).astype(jnp.bfloat16)
        keys = self.keys[:, cut]
        if self.fresh:
            new_k, _, k_scale, k_gain = self.fresh
            raw_k = new_k[:, cut].astype(jnp.float32)
            keys = jnp.concatenate([keys, (raw_k * k_scale[...] * k_gain[:, cut]).astype(jnp.bfloat16)], axis=0)
        tops = [None] * (self.rows // PIECE)
        lane = self.lane
        for begin in range(0, self.total, KEYS):
            scores = lax.dot_general(
                queries, keys[begin : begin + KEYS], (((1,), (1,)), ((), ())), preferred_element_type=jnp.float32
            )
            for index in range(len(tops)):
                piece = slice(index * PIECE, (index + 1) * PIECE)
                top = tops[index]
                for start in range(begin, min(begin + KEYS, self.total), CB):
                    column = scores[piece, start - begin : start - begin + CB]
                    if start == self.cached - CB:
                        column = jnp.where(lane < self.tail, column, NEGATIVE)
                    self.scores[slot][piece, start : start + CB] = column
                    top = column if top is None else jnp.maximum(top, column)
                tops[index] = top
        for index, top in enumerate(tops):
            piece = slice(index * PIECE, (index + 1) * PIECE)
            self.tops[slot][piece, :] = jnp.broadcast_to(jnp.max(top, axis=1, keepdims=True), (PIECE, HD))

    def soften(self, head, slot):
        top = self.tops[slot][...]
        for start in range(0, self.total, CB):
            column = self.scores[slot][:, start : start + CB]
            self.weights[slot][:, start : start + CB] = jnp.exp2(column - top).astype(jnp.bfloat16)
        self.note(top, head)

    def mix(self, head, target, lane, slot):
        cut = lanes(head)
        values = self.values[:, cut]
        if self.fresh:
            values = jnp.concatenate([values, self.fresh[1][:, cut]], axis=0)
        wide = jnp.concatenate([values, jnp.ones_like(values)], axis=1)
        mixture = jnp.dot(self.weights[slot][:, : self.total], wide, preferred_element_type=jnp.float32)
        totals = mixture[:, HD:]
        inverse = pl.reciprocal(totals, approx=True)
        inverse = inverse * (2.0 - totals * inverse)
        self.out[:, lanes(target)] = (mixture[:, :HD] * inverse).astype(jnp.bfloat16)
        self.note(totals, lane + SUM_LANE)

    def run(self, first, last, spare, ready, done, finish=None):
        ready(first, True)
        self.score(first, 0)
        count = last - first
        paired = lax.rem(count, 2) == 0

        def step(index, carry):
            head = first + 2 * index
            second = jnp.minimum(head + 1, last - 1)
            later = jnp.minimum(head + 2, last - 1)
            begun = index > 0
            before = jnp.maximum(head - 1, first)
            ready(head + 1, False)
            ready(head + 2, False)
            self.score(second, 1)
            self.soften(head, 0)
            self.mix(before, jnp.where(begun, before, spare), jnp.where(begun, before, SUM_LANE - 1), 1)
            self.score(later, 0)
            self.soften(second, 1)
            self.mix(head, head, head, 0)
            done(head).start()

            @pl.when(begun)
            def _():
                done(before).start()

            return carry

        lax.fori_loop(0, lax.shift_right_logical(count + 1, 1), step, 0)
        self.mix(last - 1, jnp.where(paired, last - 1, spare), last - 1, 1)

        @pl.when(paired)
        def _():
            done(last - 1).start()

        if finish is not None:
            finish()
        lax.fori_loop(first, last, lambda head, carry: (done(head).wait(), carry)[1], 0)


def loads(arrays, chunk, heads, sems):
    width = chunk * HD

    def copies(part):
        cut = pl.ds(pl.multiple_of(part * width, width), width)
        result = []
        for index, (source, target, rows) in enumerate(arrays):
            left = source.at[:, cut] if rows is None else source.at[rows, cut]
            right = target.at[:, cut] if rows is None else target.at[pl.ds(0, rows.size), cut]
            result.append(pltpu.make_async_copy(left, right, sems.at[index, part]))
        return result

    def start(first, last, between):
        def one(part, carry):
            for copy in copies(part):
                copy.start()
            return carry

        one(first // chunk, 0)
        between()
        lax.fori_loop(first // chunk + 1, (last + chunk - 1) // chunk, one, 0)

    def ready(first, last):
        def wait(head, at_start):
            if at_start:
                wanted = True
            else:
                wanted = (head < last) & (lax.rem(head, chunk) == 0)

            @pl.when(wanted)
            def _():
                for copy in copies(head // chunk):
                    copy.wait()

        return wait

    return start, ready


def early_kernel(facts_ref, *refs, slots, heads, chunk, sums):
    own_squares, far_squares, refs = refs[:sums], refs[sums : 2 * sums], refs[2 * sums :]
    (q_any, far_q_any, k_any, v_any, nk_any, nv_any, qg, kg, far_any, far_stat_any, own_any, stat_any) = refs[:12]
    q, k, v, nk, nv, out, stat, q_scale, k_scale, s0, s1, t0, t1, w0, w1, in_sems, out_sems, stat_sem = refs[12:]
    own_home, own_tail, held, far_tail, away = counts(facts_ref, slots)
    fresh_rows = nk.shape[0]
    scratch = ((s0, s1), (t0, t1), (w0, w1))

    def writer(target):
        def copy(head):
            return pltpu.make_async_copy(out.at[:, lanes(head)], target.at[:, lanes(head)], out_sems.at[head])

        return copy

    def write_stat(target):
        return pltpu.make_async_copy(stat, target, stat_sem)

    def far_scale():
        q_scale[...] = row_scale(total_of(far_squares, 0), HEADS * HD, SCALE)

    def own_scale():
        q_scale[...] = row_scale(total_of(own_squares, 0), HEADS * HD, SCALE)
        k_scale[...] = row_scale(total_of(own_squares, 1), HEADS * HD, 1.0)

    for count in range(1, slots):

        @pl.when(held == count)
        def _():
            size = count * CB
            rows = pl.ds(pl.multiple_of(jnp.minimum(own_home, slots - count) * CB, CB), size)
            start, ready = loads([(far_q_any, q, None), (k_any, k, rows), (v_any, v, rows)], chunk, heads, in_sems)
            start(0, heads, far_scale)
            Stage(
                q, q_scale, qg, k.at[pl.ds(0, size), :], v.at[pl.ds(0, size), :], far_tail, None, out, stat, scratch
            ).run(0, heads, heads, ready(0, heads), writer(far_any), write_stat(far_stat_any).start)
            write_stat(far_stat_any).wait()

    last = early_heads(away, heads, slots, fresh_rows // CB)

    @pl.when(last > 0)
    def _():
        start, ready = loads(
            [(q_any, q, None), (k_any, k, None), (v_any, v, None), (nk_any, nk, None), (nv_any, nv, None)],
            chunk, heads, in_sems,
        )
        start(0, last, own_scale)
        Stage(q, q_scale, qg, k, v, own_tail, (nk, nv, k_scale, kg), out, stat, scratch).run(
            0, last, heads, ready(0, last), writer(own_any), write_stat(stat_any).start
        )
        write_stat(stat_any).wait()


def late_kernel(facts_ref, *refs, slots, heads, chunk, sums):
    own_squares, refs = refs[:sums], refs[sums:]
    (q_any, k_any, v_any, nk_any, nv_any, qg, kg, _, _, own_any, stat_any) = refs[:11]
    q, k, v, nk, nv, out, stat, q_scale, k_scale, s0, s1, t0, t1, w0, w1, in_sems, out_sems, stat_sem = refs[11:]
    own_home, own_tail, held, far_tail, away = counts(facts_ref, slots)
    fresh_rows = nk.shape[0]
    scratch = ((s0, s1), (t0, t1), (w0, w1))
    first = early_heads(away, heads, slots, fresh_rows // CB)

    def own_scale():
        q_scale[...] = row_scale(total_of(own_squares, 0), HEADS * HD, SCALE)
        k_scale[...] = row_scale(total_of(own_squares, 1), HEADS * HD, 1.0)

    def writer(head):
        return pltpu.make_async_copy(out.at[:, lanes(head)], own_any.at[:, lanes(head)], out_sems.at[head])

    for count in range(1, slots + 1):

        @pl.when((own_home == count) & (first < heads))
        def _():
            rows = pl.ds(0, count * CB)
            start, ready = loads(
                [(q_any, q, None), (k_any, k, rows), (v_any, v, rows), (nk_any, nk, None), (nv_any, nv, None)],
                chunk, heads, in_sems,
            )
            start(first, heads, own_scale)

            @pl.when(first > 0)
            def _():
                copy = pltpu.make_async_copy(stat_any, stat, stat_sem)
                copy.start()
                copy.wait()

            Stage(
                q, q_scale, qg, k.at[rows, :], v.at[rows, :], own_tail, (nk, nv, k_scale, kg), out, stat, scratch
            ).run(first, heads, heads, ready(first, heads), writer)

            @pl.when(away > 0)
            def _():
                copy = pltpu.make_async_copy(stat, stat_any, stat_sem)
                copy.start()
                copy.wait()


def join_kernel(facts_ref, own_any, stat, far, far_stat, out_any, own, out, in_sems, out_sems, *, slots, step_rows):
    away = counts(facts_ref, slots)[4]
    steps = own.shape[0] // step_rows

    @pl.when(away > 0)
    def _():
        def piece(step):
            return pl.ds(pl.multiple_of(step * step_rows, step_rows), step_rows)

        def read(step):
            return pltpu.make_async_copy(own_any.at[piece(step), :], own.at[piece(step), :], in_sems.at[step])

        def write(step):
            return pltpu.make_async_copy(out.at[piece(step), :], out_any.at[piece(step), :], out_sems.at[step])

        for step in range(steps):
            read(step).start()

        def one(step, carry):
            rows = piece(step)
            near, away_stat = stat[rows, :], far_stat[rows, :]
            top = jnp.maximum(near, away_stat)
            own_part = pltpu.roll(near, HD - SUM_LANE, 1) * jnp.exp2(near - top)
            far_part = pltpu.roll(away_stat, HD - SUM_LANE, 1) * jnp.exp2(away_stat - top)
            share = far_part / (own_part + far_part)
            read(step).wait()
            for head in range(own.shape[1] // HD):
                cut = slice(head * HD, (head + 1) * HD)
                here = own[rows, cut].astype(jnp.float32)
                there = far[rows, cut].astype(jnp.float32)
                out[rows, cut] = (here + share[:, head : head + 1] * (there - here)).astype(jnp.bfloat16)
            write(step).start()
            return carry

        lax.fori_loop(0, steps, one, 0)
        for step in range(steps):
            write(step).wait()


def body(groups, tensors, new_q, new_k, new_v, cache_k, cache_v, q_gain, k_gain, cache_len, home_blocks):
    row_count, feature_count = new_q.shape
    heads = feature_count // HD
    slot_rows = cache_k.shape[0]
    slots = slot_rows // CB
    chunk = 2 if heads % 2 == 0 else 1
    half, keys = row_count, slot_rows + row_count

    far_q = lax.ppermute(new_q, "group", swap_pairs(groups))
    wide_q = new_q.astype(jnp.float32)
    wide_k = new_k.astype(jnp.float32)
    squares = jnp.stack([jnp.sum(wide_q * wide_q, axis=1), jnp.sum(wide_k * wide_k, axis=1)])
    if tensors == 2:
        squares = squares + lax.ppermute(squares, "tensor", swap_pairs(tensors))
    else:
        squares = lax.psum(squares, "tensor")
    own_squares = [squares]
    far_squares = [lax.ppermute(squares, "group", swap_pairs(groups))]
    sums = len(own_squares)

    me = lax.axis_index("group").astype(jnp.int32).reshape(1)
    q_gain = q_gain.reshape(1, feature_count)
    k_gain = k_gain.reshape(1, feature_count)
    facts = jnp.concatenate([me, cache_len, home_blocks])
    smem = [pl.BlockSpec(memory_space=pltpu.SMEM)]
    vmem = pl.BlockSpec(memory_space=pltpu.VMEM)
    anywhere = pl.BlockSpec(memory_space=pl.ANY)

    stat = jax.ShapeDtypeStruct((row_count, HD), jnp.float32)
    result = jax.ShapeDtypeStruct((row_count, feature_count), jnp.bfloat16)
    new_rows = pltpu.VMEM((row_count, feature_count), jnp.bfloat16)
    slot_space = pltpu.VMEM((slot_rows, feature_count), jnp.bfloat16)
    stat_space = pltpu.VMEM((row_count, HD), jnp.float32)
    space = [
        new_rows, slot_space, slot_space, new_rows, new_rows,
        pltpu.VMEM((row_count, feature_count + HD), jnp.bfloat16),
        stat_space, stat_space, stat_space,
        pltpu.VMEM((half, keys), jnp.float32), pltpu.VMEM((half, keys), jnp.float32),
        pltpu.VMEM((half, HD), jnp.float32), pltpu.VMEM((half, HD), jnp.float32),
        pltpu.VMEM((half, keys), jnp.bfloat16), pltpu.VMEM((half, keys), jnp.bfloat16),
        pltpu.SemaphoreType.DMA((5, heads // chunk)), pltpu.SemaphoreType.DMA((heads,)), pltpu.SemaphoreType.DMA,
    ]
    pairs = row_count * heads * CB

    def cost(blocks):
        return pl.CostEstimate(
            flops=4 * pairs * HD * blocks, bytes_accessed=4 * blocks * CB * feature_count, transcendentals=pairs * blocks
        )

    def params(size):
        return pltpu.CompilerParams(vmem_limit_bytes=size)

    far_out, far_stat, own_out, own_stat = pl.pallas_call(
        functools.partial(early_kernel, slots=slots, heads=heads, chunk=chunk, sums=sums),
        out_shape=(result, stat, result, stat),
        in_specs=smem + [vmem] * (2 * sums) + [anywhere] * 6 + [vmem] * 2,
        out_specs=(anywhere,) * 4,
        scratch_shapes=space,
        compiler_params=params(VMEM),
        cost_estimate=cost(6),
        name="early_attention",
    )(facts, *own_squares, *far_squares, new_q, far_q, cache_k, cache_v, new_k, new_v, q_gain, k_gain)
    back_out, back_stat = lax.ppermute((far_out, far_stat), "group", swap_pairs(groups))

    own_out, own_stat = pl.pallas_call(
        functools.partial(late_kernel, slots=slots, heads=heads, chunk=chunk, sums=sums),
        out_shape=(result, stat),
        in_specs=smem + [vmem] * sums + [anywhere] * 5 + [vmem] * 2 + [anywhere] * 2,
        out_specs=(anywhere,) * 2,
        scratch_shapes=space,
        input_output_aliases={8 + sums: 0, 9 + sums: 1},
        compiler_params=params(VMEM),
        cost_estimate=cost(6),
        name="late_attention",
    )(facts, *own_squares, new_q, cache_k, cache_v, new_k, new_v, q_gain, k_gain, own_out, own_stat)

    step_rows = 64
    steps = row_count // step_rows
    return pl.pallas_call(
        functools.partial(join_kernel, slots=slots, step_rows=step_rows),
        out_shape=result,
        in_specs=smem + [anywhere] + [vmem] * 3,
        out_specs=anywhere,
        scratch_shapes=[
            new_rows, new_rows, pltpu.SemaphoreType.DMA((steps,)), pltpu.SemaphoreType.DMA((steps,)),
        ],
        input_output_aliases={1: 0},
        compiler_params=params(24 * 1024 * 1024),
        name="join_parts",
    )(facts, own_out, own_stat, back_out, back_stat)


def solution(mesh):
    placed = (
        P("group", "tensor"),
        P("group", "tensor"),
        P("group", "tensor"),
        P("group", "tensor"),
        P("group", "tensor"),
        P("tensor"),
        P("tensor"),
        P(),
        P(),
    )
    return jax.shard_map(
        functools.partial(body, mesh.shape["group"], mesh.shape["tensor"]),
        mesh=mesh,
        in_specs=placed,
        out_specs=P("group", "tensor"),
        check_vma=False,
    )
```
